128 devices in a mesh: frame: 16 (over x, z), inframe: 8 (over y, core).
Axes of the slice: x: 4, y: 4, z: 4, core: 2. Of those that a mesh axis runs over, the one named last changes fastest.
Arguments:
- tokens: bfloat16 [96, 1024, 1152], P('frame', 'inframe'), may hold values from -6 to 6
- clip_ids: int32 [96], replicated, may hold values from 0 to 3, never falling along the last dimension, each value on 1 to 48 neighbouring positions
- modulation: float32 [4, 6, 1152], replicated, may hold values from -3 to 3
- w_spatial_qkv: bfloat16 [1152, 3456], replicated, may hold values from -3 to 3
- w_spatial_out: bfloat16 [1152, 1152], replicated, may hold values from -0.1875 to 0.1875
- w_temporal_qkv: bfloat16 [1152, 3456], replicated, may hold values from -3 to 3
- w_temporal_out: bfloat16 [1152, 1152], replicated, may hold values from -0.1875 to 0.1875
Outputs:
- block_out: bfloat16 [96, 1024, 1152], P('frame', 'inframe')
The draws below stay inside these ranges and needn't reach their ends.
Inputs may be any that keep to these rules, and one draw needn't show every extreme that they name: `clip_ids`: clip numbers never fall along the frames; every clip holds 1 to 48 frames, and one clip exactly that many.
All inputs are finite; a program needn't handle non-finite values.
Results may differ from the reference program's by a relative error of at most 0.0085.
Values may be sent and summed in bfloat16 or wider, within the bound.
A program may use at most 192 MiB of HBM per device.

```python
import math
import jax
import jax.numpy as jnp
import numpy as np
from jax import lax

D = 1152
HEADS = 16
S = 1024
CLIPS = 4
HD = 72
FRAMES = 96


def drawn_weight(key):
    return jax.random.truncated_normal(key, -4.0, 4.0, (D, 3 * D), jnp.float32) * D ** (-0.5)


def draw_w_spatial_qkv(key, part):
    key = jax.random.fold_in(key, 5)
    return drawn_weight(key).astype(jnp.bfloat16)


def draw_w_temporal_qkv(key, part):
    key = jax.random.fold_in(key, 9)
    return drawn_weight(key).astype(jnp.bfloat16)


def steps_of(key, shape, cuts, low, largest):
    loudness, own = 1.0, jax.random.fold_in(key, 6)
    for axis_at, shards_of in cuts:
        heights = jnp.exp(jax.random.uniform(jax.random.fold_in(own, axis_at), (shards_of,), jnp.float32, low / len(cuts), largest / len(cuts)))
        loudness = loudness * jnp.repeat(heights, shape[axis_at] // shards_of).reshape([-1 if axis == axis_at else 1 for axis in range(len(shape))])
    return loudness


def length_profile(amount, total, bound, slope):
    weights = [(1 << 20) // math.isqrt(rank ** slope) + 1 for rank in range(2, amount + 1)]
    surplus, holding = total - bound - (amount - 1), [1] * (amount - 1)
    while surplus > 0:
        movable = [i for i in range(amount - 1) if holding[i] < bound]
        whole, remaining = sum([weights[i] for i in movable]), surplus
        for i in movable:
            extra = min(bound - holding[i], max(1, remaining * weights[i] // whole), surplus)
            holding[i] = holding[i] + extra
            surplus = surplus - extra
    return np.array([bound] + holding)


def ragged(rng, amount, total, limit, slope):
    if amount == 2:
        one = jax.random.randint(rng, (), max(1, total - limit), min(limit, total - 1) + 1)
        return jnp.stack([one, total - one])
    sizes = jnp.asarray(length_profile(amount, total, limit, slope), jnp.int32)
    twos = (amount - 1) // 2
    giver, taker = sizes[1:1 + 2 * twos:2], sizes[2:2 + 2 * twos:2]
    margin = jnp.minimum(giver - 1, limit - taker)
    shifted = jax.random.randint(jax.random.fold_in(rng, 1), (twos,), 0, 1 << 20) % (margin + 1)
    sizes = sizes.at[1:1 + 2 * twos:2].set(giver - shifted).at[2:2 + 2 * twos:2].set(taker + shifted)
    return sizes[jax.random.permutation(jax.random.fold_in(rng, 2), amount)]


def bell_draw(rng, extent, width, bound, shards=(), held_as=jnp.bfloat16):
    factor_of = steps_of(rng, extent, shards, -0.22, 0.18) if shards else 1.0
    entries = jax.random.normal(rng, extent, jnp.float32) * width * factor_of
    return jnp.minimum(jnp.maximum(entries, -bound), bound).astype(held_as)


def setup_inputs(seed: int = 0) -> dict:
    seeds = jax.random.split(jax.random.key(seed), 8)
    return {
        "tokens": bell_draw(seeds[0], (FRAMES, S, D), 1.0, 6.0, ((0, 16), (1, 8))),
        "clip_ids": jnp.searchsorted(jnp.cumsum(ragged(seeds[1], CLIPS, FRAMES, FRAMES // 2, 1)), jnp.arange(FRAMES), side="right").astype(jnp.int32),
        "modulation": bell_draw(seeds[2], (CLIPS, 6, D), 0.5, 3.0, (), jnp.float32),
        "w_spatial_qkv": draw_w_spatial_qkv(jax.random.fold_in(seeds[7], 71), 0),
        "w_spatial_out": bell_draw(seeds[4], (D, D), D ** -0.5, 0.1875),
        "w_temporal_qkv": draw_w_temporal_qkv(jax.random.fold_in(seeds[7], 71), 0),
        "w_temporal_out": bell_draw(seeds[6], (D, D), D ** -0.5, 0.1875),
    }


def norm_mod(x, shift, scale):
    values = x.astype(jnp.float32)
    center = values - lax.optimization_barrier(jnp.mean(values, axis=-1, keepdims=True))
    spread = lax.optimization_barrier(jnp.mean(center * center, axis=-1, keepdims=True))
    return (center * lax.rsqrt(spread + 1e-06) * (1.0 + scale) + shift).astype(jnp.bfloat16)

def softmax_last(scores):
    top = lax.optimization_barrier(jnp.max(scores, axis=-1, keepdims=True))
    powers = jnp.exp(scores - top)
    return powers / lax.optimization_barrier(jnp.sum(powers, axis=-1, keepdims=True))

def reference(tokens, clip_ids, modulation, w_spatial_qkv, w_spatial_out, w_temporal_qkv, w_temporal_out):
    mods = modulation[clip_ids]
    factor = HD ** (-0.5)

    def spatial_frame(args):
        frame_rows, mod_rows = args
        hidden = norm_mod(frame_rows, mod_rows[0], mod_rows[1])
        qkv = jnp.dot(hidden, w_spatial_qkv, preferred_element_type=jnp.float32).astype(jnp.bfloat16)
        query = qkv[:, :D].reshape(S, HEADS, HD).astype(jnp.float32)
        keys = qkv[:, D:2 * D].reshape(S, HEADS, HD).astype(jnp.float32)
        values = qkv[:, 2 * D:].reshape(S, HEADS, HD).astype(jnp.float32)
        scores = jnp.einsum('qhe,khe->hqk', query, keys) * factor
        probs = softmax_last(scores).astype(jnp.bfloat16)
        mixed = jnp.einsum('hqk,khe->qhe', probs.astype(jnp.float32), values).astype(jnp.bfloat16).reshape(S, D)
        proj = jnp.dot(mixed, w_spatial_out, preferred_element_type=jnp.float32)
        return (frame_rows.astype(jnp.float32) + mod_rows[2] * proj).astype(jnp.bfloat16)
    first = lax.map(spatial_frame, (tokens, mods))
    block = min(S, 64)
    grouped = first.reshape(FRAMES, S // block, block, D).transpose(1, 0, 2, 3)
    same = clip_ids[:, None] == clip_ids[None, :]

    def temporal_block(rows):
        hidden = norm_mod(rows, mods[:, 3][:, None], mods[:, 4][:, None])
        qkv = jnp.dot(hidden.reshape(-1, D), w_temporal_qkv, preferred_element_type=jnp.float32).astype(jnp.bfloat16)
        qkv = qkv.reshape(FRAMES, block, 3 * D)
        query = qkv[:, :, :D].reshape(FRAMES, block, HEADS, HD).astype(jnp.float32)
        keys = qkv[:, :, D:2 * D].reshape(FRAMES, block, HEADS, HD).astype(jnp.float32)
        values = qkv[:, :, 2 * D:].reshape(FRAMES, block, HEADS, HD).astype(jnp.float32)
        scores = jnp.einsum('fphe,gphe->phfg', query, keys) * factor
        scores = jnp.where(same[None, None], scores, jnp.float32(-1e+30))
        probs = softmax_last(scores).astype(jnp.bfloat16)
        mixed = jnp.einsum('phfg,gphe->fphe', probs.astype(jnp.float32), values).astype(jnp.bfloat16)
        proj = jnp.dot(mixed.reshape(-1, D), w_temporal_out, preferred_element_type=jnp.float32).reshape(FRAMES, block, D)
        return (rows.astype(jnp.float32) + mods[:, 5][:, None] * proj).astype(jnp.bfloat16)
    result = lax.map(temporal_block, grouped)
    return result.transpose(1, 0, 2, 3).reshape(FRAMES, S, D)
```

```python
import functools
import math

import jax
import jax.numpy as jnp
from jax import lax
from jax.experimental import pallas as pl
from jax.experimental.pallas import tpu as pltpu
from jax.sharding import PartitionSpec as P

MESH = pl.DeviceIdType.MESH
F32, BF16 = jnp.float32, jnp.bfloat16
HEADS = 16
HD = 72
D = HEADS * HD
WIN = 256
LOG2E = 1.0 / math.log(2.0)
NEG = -1e30


def normed(x, shift, scale):
    center = x - jnp.mean(x, axis=-1, keepdims=True)
    spread = jnp.mean(center * center, axis=-1, keepdims=True)
    return (center * lax.rsqrt(spread + 1e-06) * (1.0 + scale) + shift).astype(BF16)


def dot(a, b):
    return jnp.dot(a, b, preferred_element_type=F32)


def dot_t(a, b):
    return lax.dot_general(a, b, (((1,), (1,)), ((), ())), preferred_element_type=F32)


def kernel(
    tokens, clips, mod, wsq, wso, wtq, wto,
    final,
    xin, wq, wo, wo2, q_s, kt_s, v_s, mixed, first_out, recv_t, f32_t, rows_t, qkv_t, mixed_t, out_t,
    mods_t,
    send_a, recv_a, send_b, recv_b, send_c, recv_c, w_sem, all_in,
):
    i = lax.axis_index("frame")
    j = lax.axis_index("inframe")
    x, z = i // 4, i % 4
    y = j // 2
    parity = (x + z) % 2

    def owner_of(l):
        return l + (1 - parity) * ((l + 1) // 4) + parity * ((l + 2) // 3)

    own = jnp.where(parity == 0, j - j // 4, j - (j + 2) // 4)
    idle = jnp.where(parity == 0, j % 4 == 3, j % 4 == 1)
    owner = jnp.logical_not(idle)
    frame = i * 6 + own

    def weight_copy(src, dst, n):
        return pltpu.make_async_copy(src, dst, w_sem.at[n])

    barrier = pltpu.get_barrier_semaphore()

    @pl.loop(1, 8)
    def _(k):
        pl.semaphore_signal(barrier, inc=1, device_id=(i, (j + k) % 8), device_id_type=MESH)

    @pl.loop(1, 16)
    def _(k):
        pl.semaphore_signal(barrier, inc=1, device_id=((i + k) % 16, j), device_id_type=MESH)

    weight_copy(wsq, wq, 0).start()
    weight_copy(wso, wo, 1).start()
    weight_copy(wto, wo2, 2).start()
    pl.semaphore_wait(barrier, 22)

    def token_copy(l, dest):
        return pltpu.make_async_remote_copy(
            src_ref=tokens.at[l], dst_ref=xin.at[j], send_sem=send_a, recv_sem=recv_a.at[j],
            device_id=(i, dest), device_id_type=MESH,
        )

    @pl.loop(0, 6)
    def _(l):
        dest = owner_of(l)

        @pl.when(dest != j)
        def _():
            token_copy(l, dest).start()

    @pl.when(owner)
    def _():
        pltpu.make_async_copy(tokens.at[own], xin.at[j], recv_a.at[j]).start()

    @pl.loop(1, 8)
    def _(k):
        pl.semaphore_signal(all_in, inc=1, device_id=(i, (j + k) % 8), device_id_type=MESH)

    clip_row = clips[...]
    row_id = lax.broadcasted_iota(jnp.int32, (96, 96), 0)
    col_id = lax.broadcasted_iota(jnp.int32, (96, 96), 1)
    clip_rows = jnp.broadcast_to(clip_row, (96, 96))
    clip_col = jnp.sum(jnp.where(row_id == col_id, clip_rows, 0), axis=1, keepdims=True)

    @pl.loop(0, 3)
    def _(n):
        picked = jnp.zeros((96, D), F32)
        for c in range(4):
            picked = jnp.where(clip_col == c, mod[c, pl.ds(3 + n, 1), :], picked)
        mods_t[n] = picked

    weight_copy(wsq, wq, 0).wait()
    weight_copy(wso, wo, 1).wait()
    weight_copy(wto, wo2, 2).wait()

    @pl.when(owner)
    def _():
        lane96 = lax.broadcasted_iota(jnp.int32, (1, 96), 1)
        own_clip = jnp.sum(jnp.where(lane96 == frame, clip_row, 0), axis=1, keepdims=True)

        def own_mod(n):
            picked = jnp.zeros((1, D), F32)
            for c in range(4):
                picked = jnp.where(own_clip == c, mod[c, n : n + 1, :], picked)
            return picked

        shift, scale = own_mod(0), own_mod(1)

        @pl.loop(0, 4)
        def _(s):
            yy = (y + (s + 1) // 2 * (1 - s % 2 * 2) + 4) % 4
            for c in range(2):
                pltpu.make_async_copy(tokens.at[0], xin.at[yy * 2 + c], recv_a.at[yy * 2 + c]).wait()
            rows = xin[pl.ds(2 * yy, 2)].astype(F32).reshape(256, D)
            hidden = normed(rows, shift, scale)
            q = dot(hidden, wq[:, :D]) * (LOG2E * HD**-0.5)
            q_s[pl.ds(2 * yy, 2)] = q.astype(BF16).reshape(2, 128, D)
            k = dot(hidden, wq[:, D : 2 * D])
            kt_s[:, pl.ds(pl.multiple_of(yy * 256, 256), 256)] = k.T.astype(BF16)
            v = dot(hidden, wq[:, 2 * D :])
            v_s[pl.ds(pl.multiple_of(yy * 256, 256), 256), :] = v.astype(BF16)

    weight_copy(wtq, wq, 3).start()
    pl.semaphore_wait(all_in, 7)

    @pl.when(owner)
    def _():
        lane96 = lax.broadcasted_iota(jnp.int32, (1, 96), 1)
        own_clip = jnp.sum(jnp.where(lane96 == frame, clip_row, 0), axis=1, keepdims=True)
        gate = jnp.zeros((1, D), F32)
        for c in range(4):
            gate = jnp.where(own_clip == c, mod[c, 2:3, :], gate)

        @pl.loop(0, 4)
        def _(s):
            t = (x + 2 + 3 * s) % 4
            rows = pl.ds(pl.multiple_of(t * 32, 32), 32)

            def head(h):
                at = jnp.minimum(h * HD // 128, 7)
                off = pl.multiple_of(at * 128, 128)
                lane = lax.broadcasted_iota(jnp.int32, (1, WIN), 1) + (at * 128 - h * HD)
                inside = jnp.logical_and(lane >= 0, lane < HD)
                q = q_s[:, rows, pl.ds(off, WIN)].reshape(256, WIN)
                q = jnp.where(inside, q, jnp.zeros_like(q))
                scores = dot(q, kt_s[pl.ds(off, WIN), :])
                powers = jnp.exp2(scores - jnp.max(scores, axis=-1, keepdims=True))
                total = jnp.sum(powers, axis=-1, keepdims=True)
                out = dot(powers.astype(BF16), v_s[:, pl.ds(off, WIN)]) / total
                mixed[:, pl.ds(off, WIN)] = jnp.where(inside, out, mixed[:, pl.ds(off, WIN)])

            @pl.loop(0, HEADS // 2)
            def _(u):
                head(2 * u)
                head(2 * u + 1)

            proj = dot(mixed[...].astype(BF16), wo[...])
            base = xin[:, rows, :].astype(F32).reshape(256, D)
            first = base + gate * proj
            first_out[:, pl.ds(t * 4, 4)] = first.reshape(8, 4, 8, D).astype(BF16)

            @pl.loop(0, 32)
            def _(n):
                dj, di = n // 4, t * 4 + n % 4

                @pl.when(jnp.logical_or(dj != j, di != i))
                def _():
                    pltpu.make_async_remote_copy(
                        src_ref=first_out.at[dj, di], dst_ref=recv_t.at[frame], send_sem=send_b,
                        recv_sem=recv_b, device_id=(di, dj), device_id_type=MESH,
                    ).start()

        pltpu.make_async_copy(first_out.at[j, i], recv_t.at[frame], recv_b).start()

    weight_copy(wtq, wq, 3).wait()
    pltpu.make_async_copy(recv_t, recv_t, recv_b).wait()

    @pl.loop(0, 12)
    def _(c):
        rows = recv_t[pl.ds(c * 8, 8)].astype(F32).reshape(64, D)
        for b in range(9):
            f32_t[b, pl.ds(pl.multiple_of(c * 64, 64), 64), :] = rows[:, b * 128 : b * 128 + 128]

    @pl.loop(0, 8)
    def _(p):
        rows = jnp.concatenate([f32_t[b, pl.ds(p, 96, stride=8), :] for b in range(9)], axis=1)
        rows_t[pl.ds(pl.multiple_of(p * 96, 96), 96), :] = normed(rows, mods_t[0], mods_t[1])

    @pl.loop(0, 3)
    def _(c):
        at = pl.ds(pl.multiple_of(c * 256, 256), 256)
        hidden = rows_t[at, :]
        q = dot(hidden, wq[:, :D]) * (LOG2E * HD**-0.5)
        qkv_t[at, :D] = q.astype(BF16)
        qkv_t[at, D : 2 * D] = dot(hidden, wq[:, D : 2 * D]).astype(BF16)
        qkv_t[at, 2 * D :] = dot(hidden, wq[:, 2 * D :]).astype(BF16)

    same = clip_col == clip_rows

    @pl.loop(0, 8)
    def _(p):
        at = pl.ds(pl.multiple_of(p * 96, 96), 96)
        for h in range(HEADS):
            off = min(h * HD // 128, 7) * 128
            lane = lax.broadcasted_iota(jnp.int32, (1, WIN), 1) + (off - h * HD)
            inside = jnp.logical_and(lane >= 0, lane < HD)
            q = qkv_t[at, off : off + WIN]
            q = jnp.where(inside, q, jnp.zeros_like(q))
            scores = dot_t(q, qkv_t[at, D + off : D + off + WIN])
            scores = jnp.where(same, scores, NEG)
            powers = jnp.exp2(scores - jnp.max(scores, axis=-1, keepdims=True))
            total = jnp.sum(powers, axis=-1, keepdims=True)
            out = dot(powers.astype(BF16), qkv_t[at, 2 * D + off : 2 * D + off + WIN]) / total
            mixed_t[at, off : off + WIN] = jnp.where(inside, out, mixed_t[at, off : off + WIN])

    @pl.loop(0, 4)
    def _(c):
        proj = dot(mixed_t[pl.ds(pl.multiple_of(c * 192, 192), 192), :].astype(BF16), wo2[...])
        for n in range(2):
            at = pl.ds(c * 2 + n, 96, stride=8)
            for b in range(9):
                cols = slice(b * 128, b * 128 + 128)
                f32_t[b, at, :] = f32_t[b, at, :] + mods_t[2, :, cols] * proj[n * 96 : n * 96 + 96, cols]

    @pl.loop(0, 12)
    def _(c):
        at = pl.ds(pl.multiple_of(c * 64, 64), 64)
        rows = jnp.concatenate([f32_t[b, at, :] for b in range(9)], axis=1)
        out_t[pl.ds(c * 8, 8)] = rows.reshape(8, 8, D).astype(BF16)

    @pl.loop(1, 16)
    def _(k):
        di = (i + k) % 16
        pltpu.make_async_remote_copy(
            src_ref=out_t.at[pl.ds(di * 6, 6)], dst_ref=final.at[i], send_sem=send_c,
            recv_sem=recv_c, device_id=(di, j), device_id_type=MESH,
        ).start()

    pltpu.make_async_copy(out_t.at[pl.ds(i * 6, 6)], final.at[i], recv_c).start()

    @pl.loop(0, 6)
    def _(l):
        dest = owner_of(l)

        @pl.when(dest != j)
        def _():
            token_copy(l, dest).wait_send()

    @pl.when(owner)
    def _():
        @pl.loop(0, 127)
        def _(n):
            pltpu.make_async_copy(first_out.at[0, 0], recv_t.at[0], send_b).wait()

    @pl.loop(0, 15)
    def _(n):
        pltpu.make_async_copy(out_t.at[pl.ds(0, 6)], out_t.at[pl.ds(0, 6)], send_c).wait()

    pltpu.make_async_copy(final, final, recv_c).wait()


def body(tokens, clip_ids, modulation, w_spatial_qkv, w_spatial_out, w_temporal_qkv, w_temporal_out):
    any_, vmem = pl.BlockSpec(memory_space=pl.ANY), pl.BlockSpec(memory_space=pltpu.VMEM)
    dma = pltpu.SemaphoreType.DMA
    final = pl.pallas_call(
        kernel,
        out_shape=jax.ShapeDtypeStruct((16, 6, 8, D), BF16),
        in_specs=[any_, vmem, vmem, any_, any_, any_, any_],
        out_specs=any_,
        scratch_shapes=[
            pltpu.VMEM((8, 128, D), BF16),
            pltpu.VMEM((D, 3 * D), BF16),
            pltpu.VMEM((D, D), BF16),
            pltpu.VMEM((D, D), BF16),
            pltpu.VMEM((8, 128, D), BF16),
            pltpu.VMEM((D, 1024), BF16),
            pltpu.VMEM((1024, D), BF16),
            pltpu.VMEM((256, D), F32),
            pltpu.VMEM((8, 16, 8, D), BF16),
            pltpu.VMEM((96, 8, D), BF16),
            pltpu.VMEM((9, 768, 128), F32),
            pltpu.VMEM((768, D), BF16),
            pltpu.VMEM((768, 3 * D), BF16),
            pltpu.VMEM((768, D), F32),
            pltpu.VMEM((96, 8, D), BF16),
            pltpu.VMEM((3, 96, D), F32),
            dma, dma((8,)), dma, dma, dma, dma, dma((4,)),
            pltpu.SemaphoreType.REGULAR,
        ],
        compiler_params=pltpu.CompilerParams(
            collective_id=0, has_side_effects=True, vmem_limit_bytes=60 * 1024 * 1024
        ),
        name="block",
    )(tokens, clip_ids.reshape(1, 96), modulation, w_spatial_qkv, w_spatial_out, w_temporal_qkv, w_temporal_out)
    return final.transpose(1, 0, 2, 3).reshape(6, 128, D)


def solution(mesh):
    in_specs = (P("frame", "inframe", None), P(), P(), P(), P(), P(), P())
    out_specs = P("frame", "inframe", None)
    return jax.shard_map(body, mesh=mesh, in_specs=in_specs, out_specs=out_specs, check_vma=False)
```

```python
import math

import jax
import jax.numpy as jnp
from jax import lax
from jax.experimental import pallas as pl
from jax.experimental.pallas import tpu as pltpu
from jax.sharding import PartitionSpec as P

MESH = pl.DeviceIdType.MESH
F32, BF16 = jnp.float32, jnp.bfloat16
HEADS = 16
HD = 72
D = HEADS * HD
WIN = 256
Q_SCALE = HD**-0.5 / math.log(2.0)
NEG = -1e30


def hops(*offsets):
    return sum(min(o, 4 - o) for o in offsets)


YZ_FAR_FIRST = sorted(((dy, dz) for dy in range(4) for dz in range(4)), key=lambda o: -hops(*o))


def normed(x, shift, scale):
    center = x - jnp.mean(x, axis=-1, keepdims=True)
    spread = jnp.mean(center * center, axis=-1, keepdims=True)
    return (center * lax.rsqrt(spread + 1e-06) * (1.0 + scale) + shift).astype(BF16)


def dot(a, b):
    return jnp.dot(a, b, preferred_element_type=F32)


def dot_t(a, b):
    return lax.dot_general(a, b, (((1,), (1,)), ((), ())), preferred_element_type=F32)


def window(h):
    return min(h * HD // 128, 7) * 128


def kernel(
    tokens, clips, mod, wsq, wso, wtq, wto,
    final,
    xin, wq, wo, wo2, qt_s, k_s, vt_s, score, power, mixt, first_out, recv_t, f32_t, rows_t, qkv_t, out_t, mods_t,
    send_a, recv_a, send_b, recv_b, send_c, recv_c, w_sem, all_in,
):
    i = lax.axis_index("frame")
    j = lax.axis_index("inframe")
    x, z = i // 4, i % 4
    y, core = j // 2, j % 2
    parity = (x + z) % 2

    def owned(dev):
        return jnp.where(parity == 0, dev - dev // 4, dev - (dev + 2) // 4)

    def owns(dev):
        return jnp.where(parity == 0, dev % 4 != 3, dev % 4 != 1)

    own, owner = owned(j), owns(j)
    frame = i * 6 + own

    def weight_copy(src, dst, n):
        return pltpu.make_async_copy(src, dst, w_sem.at[n])

    barrier = pltpu.get_barrier_semaphore()

    @pl.loop(1, 8)
    def _(k):
        pl.semaphore_signal(barrier, inc=1, device_id=(i, (j + k) % 8), device_id_type=MESH)

    @pl.loop(1, 16)
    def _(k):
        pl.semaphore_signal(barrier, inc=1, device_id=((i + k) % 16, j), device_id_type=MESH)

    weight_copy(wsq, wq, 0).start()
    weight_copy(wso, wo, 1).start()
    weight_copy(wto, wo2, 2).start()
    pl.semaphore_wait(barrier, 22)

    def token_copy(dest):
        return pltpu.make_async_remote_copy(
            src_ref=tokens.at[owned(dest)], dst_ref=xin.at[j], send_sem=send_a, recv_sem=recv_a.at[j],
            device_id=(i, dest), device_id_type=MESH,
        )

    others = [(dy, dc) for dy in (2, 1, 3, 0) for dc in (0, 1) if (dy, dc) != (0, 0)]
    for dy, dc in others:
        dest = (y + dy) % 4 * 2 + (core + dc) % 2

        @pl.when(owns(dest))
        def _(dest=dest):
            token_copy(dest).start()

    @pl.when(owner)
    def _():
        pltpu.make_async_copy(tokens.at[own], xin.at[j], recv_a.at[j]).start()

    @pl.loop(1, 8)
    def _(k):
        pl.semaphore_signal(all_in, inc=1, device_id=(i, (j + k) % 8), device_id_type=MESH)

    def frame_at(slot):
        step = slot // 48 + 1 + slot % 48 // 24 * 2
        return (x + 4 - step % 4) % 4 * 24 + slot % 24

    clip_row = clips[...]
    row_id = lax.broadcasted_iota(jnp.int32, (96, 96), 0)
    col_id = lax.broadcasted_iota(jnp.int32, (96, 96), 1)
    clip_rows = jnp.broadcast_to(clip_row, (96, 96))
    clip_natural = jnp.sum(jnp.where(row_id == col_id, clip_rows, 0), axis=1, keepdims=True)
    clip_col = jnp.sum(jnp.where(frame_at(row_id) == col_id, clip_rows, 0), axis=1, keepdims=True)
    clip_slots = jnp.sum(jnp.where(row_id == frame_at(col_id), clip_natural, 0), axis=0, keepdims=True)

    @pl.loop(0, 3)
    def _(n):
        picked = jnp.zeros((96, D), F32)
        for c in range(4):
            picked = jnp.where(clip_col == c, mod[3 + n, c : c + 1, :], picked)
        mods_t[n] = picked

    lane96 = lax.broadcasted_iota(jnp.int32, (1, 96), 1)
    own_clip = jnp.sum(jnp.where(lane96 == frame, clip_row, 0), axis=1, keepdims=True)

    def own_mod(n):
        picked = jnp.zeros((1, D), F32)
        for c in range(4):
            picked = jnp.where(own_clip == c, mod[n, c : c + 1, :], picked)
        return picked

    vt_s[:, HD:, :] = jnp.ones((HEADS, 8, 1024), BF16)

    weight_copy(wsq, wq, 0).wait()
    weight_copy(wso, wo, 1).wait()
    weight_copy(wto, wo2, 2).wait()

    @pl.when(owner)
    def _():
        shift, scale = own_mod(0), own_mod(1)

        @pl.loop(0, 4)
        def _(s):
            yy = (y + jnp.where(s == 0, 0, jnp.where(s == 1, 2, jnp.where(s == 2, 1, 3)))) % 4
            for c in range(2):
                pltpu.make_async_copy(tokens.at[0], xin.at[yy * 2 + c], recv_a.at[yy * 2 + c]).wait()
            rows = xin[pl.ds(2 * yy, 2)].astype(F32).reshape(256, D)
            hidden = normed(rows, shift, scale)
            at = pl.ds(pl.multiple_of(yy * 256, 256), 256)
            q = (dot(hidden, wq[:, :D]) * Q_SCALE).reshape(2, 2, 2, 32, D)
            for par in range(2):
                qt = q[:, :, par].reshape(128, D).T
                cols = pl.ds(pl.multiple_of(par * 512 + yy * 128, 128), 128)
                for h in range(HEADS):
                    off = window(h)
                    row = lax.broadcasted_iota(jnp.int32, (WIN, 1), 0) + (off - h * HD)
                    inside = jnp.logical_and(row >= 0, row < HD)
                    qt_s[h, :, cols] = jnp.where(inside, qt[off : off + WIN], 0.0).astype(BF16)
            k_s[at, :] = dot(hidden, wq[:, D : 2 * D]).astype(BF16)
            v = dot(hidden, wq[:, 2 * D :])
            vt_s[:, :HD, at] = v.T.reshape(HEADS, HD, 256).astype(BF16)

    weight_copy(wtq, wq, 3).start()
    pl.semaphore_wait(all_in, 7)

    @pl.when(owner)
    def _():
        gate = own_mod(2)

        @pl.loop(0, 2)
        def _(s):
            par = (x + 1 + s) % 2
            cols = pl.ds(pl.multiple_of(par * 512, 512), 512)

            def scores(h, n):
                off = pl.multiple_of(jnp.minimum(h * HD // 128, 7) * 128, 128)
                score[n] = dot(k_s[:, pl.ds(off, WIN)], qt_s[h, :, cols])

            def attend(h, n):
                values = score[n]
                top = jnp.max(values, axis=0, keepdims=True)
                power[n] = jnp.exp2(values - top).astype(BF16)
                out = dot(vt_s[h], power[n])
                mixt[pl.ds(pl.multiple_of(h * HD, 8), HD), :] = out[:HD] * (1.0 / out[HD : HD + 1])

            scores(0, 0)

            @pl.loop(0, HEADS // 2)
            def _(u):
                scores(2 * u + 1, 1)
                attend(2 * u, 0)
                scores(jnp.minimum(2 * u + 2, HEADS - 1), 0)
                attend(2 * u + 1, 1)

            @pl.loop(0, 2)
            def _(b):
                mixed = mixt[:, pl.ds(pl.multiple_of(b * 256, 256), 256)].T.astype(BF16)
                proj = dot(mixed, wo[...]).reshape(4, 2, 32, D)
                devs = pl.ds(4 * b, 4)
                for a in range(2):
                    at = pl.ds(pl.multiple_of(a * 64 + par * 32, 32), 32)
                    first = xin[devs, at, :].astype(F32) + gate * proj[:, a]
                    first_out[devs, pl.ds(8 * a + 4 * par, 4)] = first.reshape(4, 4, 8, D).astype(BF16)

            for dy, dz in YZ_FAR_FIRST:
                for dc in range(2):
                    for k in range(2):
                        dx = (1 + s + 2 * k) % 4
                        di = (x + dx) % 4 * 4 + (z + dz) % 4
                        dj = (y + dy) % 4 * 2 + (core + dc) % 2
                        slot = (s * 2 + k) * 24 + z * 6 + own
                        copy = pltpu.make_async_remote_copy(
                            src_ref=first_out.at[dj, di], dst_ref=recv_t.at[slot], send_sem=send_b,
                            recv_sem=recv_b.at[s], device_id=(di, dj), device_id_type=MESH,
                        )
                        if (dy, dz, dc, k) != (0, 0, 0, 1):
                            copy.start()
                        else:
                            pl.when(s == 0)(copy.start)

        pltpu.make_async_copy(first_out.at[j, i], recv_t.at[72 + z * 6 + own], recv_b.at[1]).start()

    weight_copy(wtq, wq, 3).wait()

    @pl.loop(0, 2)
    def _(s):
        slots = recv_t.at[pl.ds(48 * s, 48)]
        pltpu.make_async_copy(slots, slots, recv_b.at[s]).wait()

        @pl.loop(0, 6)
        def _(c):
            rows = recv_t[pl.ds(48 * s + c * 8, 8)].astype(F32).reshape(64, D)
            for b in range(9):
                f32_t[b, pl.ds(pl.multiple_of(s * 384 + c * 64, 64), 64), :] = rows[:, b * 128 : b * 128 + 128]

        half = pl.ds(pl.multiple_of(48 * s, 48), 48)

        @pl.loop(0, 8)
        def _(p):
            rows = jnp.concatenate([f32_t[b, pl.ds(s * 384 + p, 48, stride=8), :] for b in range(9)], axis=1)
            at = pl.ds(pl.multiple_of(p * 48, 48), 48)
            rows_t[s, at, :] = normed(rows, mods_t[0, half, :], mods_t[1, half, :])

        hidden = rows_t[s]
        qkv_t[s, :, :D] = (dot(hidden, wq[:, :D]) * Q_SCALE).astype(BF16)
        qkv_t[s, :, D : 2 * D] = dot(hidden, wq[:, D : 2 * D]).astype(BF16)
        qkv_t[s, :, 2 * D :] = dot(hidden, wq[:, 2 * D :]).astype(BF16)

    same = clip_col == clip_slots

    @pl.loop(0, 8)
    def _(p):
        at = pl.ds(pl.multiple_of(p * 48, 48), 48)
        blocks = [jnp.zeros((96, 128), F32) for _ in range(9)]
        for h in range(HEADS):
            off = window(h)
            lane = lax.broadcasted_iota(jnp.int32, (1, WIN), 1) + (off - h * HD)
            inside = jnp.logical_and(lane >= 0, lane < HD)

            def part(n):
                cols = slice(n * D + off, n * D + off + WIN)
                return jnp.concatenate([qkv_t[0, at, cols], qkv_t[1, at, cols]], axis=0)

            q = part(0)
            q = jnp.where(inside, q, jnp.zeros_like(q))
            scores = jnp.where(same, dot_t(q, part(1)), NEG)
            powers = jnp.exp2(scores - jnp.max(scores, axis=-1, keepdims=True))
            total = jnp.sum(powers, axis=-1, keepdims=True)
            out = dot(powers.astype(BF16), part(2)) * (1.0 / total)
            for b in range(off // 128, off // 128 + 2):
                lanes = slice(b * 128 - off, b * 128 - off + 128)
                blocks[b] = jnp.where(inside[:, lanes], out[:, lanes], blocks[b])
        for b in range(9):
            cols = slice(b * 128, b * 128 + 128)
            rows_t[0, at, cols] = blocks[b][:48].astype(BF16)
            rows_t[1, at, cols] = blocks[b][48:].astype(BF16)

    def back_copy(s, k, dz):
        dx = (4 - (1 + s + 2 * k)) % 4
        di = (x + dx) % 4 * 4 + (z + dz) % 4
        slot = (s * 2 + k) * 24 + (z + dz) % 4 * 6
        return di, out_t.at[pl.ds(slot, 6)]

    for s in range(2):
        proj = dot(rows_t[s], wo2[...])
        for p in range(8):
            at = pl.ds(s * 384 + p, 48, stride=8)
            for b in range(9):
                cols = slice(b * 128, b * 128 + 128)
                f32_t[b, at, :] = f32_t[b, at, :] + mods_t[2, s * 48 : s * 48 + 48, cols] * proj[p * 48 : p * 48 + 48, cols]

        @pl.loop(0, 6)
        def _(c, s=s):
            at = pl.ds(pl.multiple_of(s * 384 + c * 64, 64), 64)
            rows = jnp.concatenate([f32_t[b, at, :] for b in range(9)], axis=1)
            out_t[pl.ds(s * 48 + c * 8, 8)] = rows.reshape(8, 8, D).astype(BF16)

        for dz in (2, 1, 3, 0):
            for k in range(2):
                di, src = back_copy(s, k, dz)
                if (s, k, dz) == (1, 1, 0):
                    pltpu.make_async_copy(src, final.at[:, i], recv_c).start()
                else:
                    pltpu.make_async_remote_copy(
                        src_ref=src, dst_ref=final.at[:, i], send_sem=send_c, recv_sem=recv_c,
                        device_id=(di, j), device_id_type=MESH,
                    ).start()

    for dy, dc in others:
        dest = (y + dy) % 4 * 2 + (core + dc) % 2

        @pl.when(owns(dest))
        def _(dest=dest):
            token_copy(dest).wait_send()

    @pl.when(owner)
    def _():
        @pl.loop(0, 127)
        def _(n):
            pltpu.make_async_copy(first_out.at[0, 0], recv_t.at[0], send_b).wait()

    @pl.loop(0, 15)
    def _(n):
        pltpu.make_async_copy(out_t.at[pl.ds(0, 6)], out_t.at[pl.ds(0, 6)], send_c).wait()

    pltpu.make_async_copy(final, final, recv_c).wait()


def body(tokens, clip_ids, modulation, w_spatial_qkv, w_spatial_out, w_temporal_qkv, w_temporal_out):
    any_, vmem = pl.BlockSpec(memory_space=pl.ANY), pl.BlockSpec(memory_space=pltpu.VMEM)
    dma = pltpu.SemaphoreType.DMA
    final = pl.pallas_call(
        kernel,
        out_shape=jax.ShapeDtypeStruct((6, 16, 8, D), BF16),
        in_specs=[any_, vmem, vmem, any_, any_, any_, any_],
        out_specs=any_,
        scratch_shapes=[
            pltpu.VMEM((8, 128, D), BF16),
            pltpu.VMEM((D, 3 * D), BF16),
            pltpu.VMEM((D, D), BF16),
            pltpu.VMEM((D, D), BF16),
            pltpu.VMEM((HEADS, WIN, 1024), BF16),
            pltpu.VMEM((1024, D), BF16),
            pltpu.VMEM((HEADS, HD + 8, 1024), BF16),
            pltpu.VMEM((2, 1024, 512), F32),
            pltpu.VMEM((2, 1024, 512), BF16),
            pltpu.VMEM((D, 512), F32),
            pltpu.VMEM((8, 16, 8, D), BF16),
            pltpu.VMEM((96, 8, D), BF16),
            pltpu.VMEM((9, 768, 128), F32),
            pltpu.VMEM((2, 384, D), BF16),
            pltpu.VMEM((2, 384, 3 * D), BF16),
            pltpu.VMEM((96, 8, D), BF16),
            pltpu.VMEM((3, 96, D), F32),
            dma, dma((8,)), dma, dma((2,)), dma, dma, dma((4,)),
            pltpu.SemaphoreType.REGULAR,
        ],
        compiler_params=pltpu.CompilerParams(
            collective_id=0, has_side_effects=True, vmem_limit_bytes=63 * 1024 * 1024
        ),
        name="block",
    )(
        tokens, clip_ids.reshape(1, 96), modulation.transpose(1, 0, 2),
        w_spatial_qkv, w_spatial_out, w_temporal_qkv, w_temporal_out,
    )
    return final.reshape(6, 128, D)


def solution(mesh):
    in_specs = (P("frame", "inframe", None), P(), P(), P(), P(), P(), P())
    out_specs = P("frame", "inframe", None)
    return jax.shard_map(body, mesh=mesh, in_specs=in_specs, out_specs=out_specs, check_vma=False)
```

```python
import math

import jax
import jax.numpy as jnp
from jax import lax
from jax.experimental import pallas as pl
from jax.experimental.pallas import tpu as pltpu
from jax.sharding import PartitionSpec as P

MESH = pl.DeviceIdType.MESH
F32, BF16 = jnp.float32, jnp.bfloat16
HEADS = 16
HALF = 8
HD = 72
D = HEADS * HD
WIN = 256
WIDE = 640
Q_SCALE = HD**-0.5 / math.log(2.0)
NEG = -1e30


def hops(*offsets):
    return sum(min(o, 4 - o) for o in offsets)


YZ_FAR_FIRST = sorted(((dy, dz) for dy in range(4) for dz in range(4)), key=lambda o: -hops(*o))
XZ_FAR_FIRST = YZ_FAR_FIRST[:-1]


def normed(x, shift, scale):
    center = x - jnp.mean(x, axis=-1, keepdims=True)
    spread = jnp.mean(center * center, axis=-1, keepdims=True)
    return (center * lax.rsqrt(spread + 1e-06) * (1.0 + scale) + shift).astype(BF16)


def dot(a, b):
    return jnp.dot(a, b, preferred_element_type=F32)


def dot_t(a, b):
    return lax.dot_general(a, b, (((1,), (1,)), ((), ())), preferred_element_type=F32)


def window(h):
    return min(h * HD // 128, 7) * 128


def kernel(
    tokens, clips, mod, wsq, wso, wtq, wto,
    final,
    xin, wq, wo, wo2, qtf, vtf, qt_s, k_s, vt_s, score, power, mixt, mix_out, mix_all, first_out, recv_t, f32_t,
    rows_a, rows_b, qkv_a, qkv_b, out_t, mods_t,
    send_a, recv_a, send_m, recv_m, send_b, recv_b, send_c, recv_c, w_sem, all_in,
):
    i = lax.axis_index("frame")
    j = lax.axis_index("inframe")
    x, z = i // 4, i % 4
    y, core = j // 2, j % 2
    parity = (x + z) % 2
    sibling = y * 2 + 1 - core

    count = 2 - (y + parity) % 2

    def weight_copy(src, dst, n):
        return pltpu.make_async_copy(src, dst, w_sem.at[n])

    barrier = pltpu.get_barrier_semaphore()

    @pl.loop(1, 8)
    def _(k):
        pl.semaphore_signal(barrier, inc=1, device_id=(i, (j + k) % 8), device_id_type=MESH)

    @pl.loop(1, 16)
    def _(k):
        pl.semaphore_signal(barrier, inc=1, device_id=((i + k) % 16, j), device_id_type=MESH)

    weight_copy(wsq, wq, 0).start()
    weight_copy(wso, wo, 1).start()
    weight_copy(wto, wo2, 2).start()
    pl.semaphore_wait(barrier, 22)

    def token_copy(src, f, block, dest):
        return pltpu.make_async_remote_copy(
            src_ref=src, dst_ref=xin.at[f, block], send_sem=send_a, recv_sem=recv_a.at[f, block],
            device_id=(i, dest), device_id_type=MESH,
        )

    for dy in (2, 1, 3):
        token_copy(tokens.at[(y + dy) % 4], 0, j, (y + dy) % 4 * 2 + core).start()
    token_copy(tokens.at[y], 0, j, sibling).start()
    pltpu.make_async_copy(tokens.at[y], xin.at[0, j], recv_a.at[0, j]).start()
    for e in range(2):
        chip = parity + 2 * e

        @pl.when(chip != y)
        def _(e=e, chip=chip):
            token_copy(tokens.at[4 + e], 1, j, chip * 2 + core).start()

        @pl.when(chip == y)
        def _(e=e):
            token_copy(tokens.at[4 + e], 1, j, sibling).start()
            pltpu.make_async_copy(tokens.at[4 + e], xin.at[1, j], recv_a.at[1, j]).start()

    @pl.loop(1, 8)
    def _(k):
        pl.semaphore_signal(all_in, inc=1, device_id=(i, (j + k) % 8), device_id_type=MESH)

    def frame_at(slot):
        late = slot - 64
        return jnp.where(slot < 64, slot // 4 * 6 + slot % 4, late // 2 * 6 + 4 + late % 2)

    clip_row = clips[...]
    row_id = lax.broadcasted_iota(jnp.int32, (96, 96), 0)
    col_id = lax.broadcasted_iota(jnp.int32, (96, 96), 1)
    clip_rows = jnp.broadcast_to(clip_row, (96, 96))
    clip_natural = jnp.sum(jnp.where(row_id == col_id, clip_rows, 0), axis=1, keepdims=True)
    clip_col = jnp.sum(jnp.where(frame_at(row_id) == col_id, clip_rows, 0), axis=1, keepdims=True)
    clip_slots = jnp.sum(jnp.where(row_id == frame_at(col_id), clip_natural, 0), axis=0, keepdims=True)

    @pl.loop(0, 3)
    def _(n):
        picked = jnp.zeros((96, D), F32)
        for c in range(4):
            picked = jnp.where(clip_col == c, mod[3 + n, c : c + 1, :], picked)
        mods_t[n] = picked

    vt_s[:, HD:, :] = jnp.ones((HALF, 8, 1024), BF16)

    weight_copy(wsq, wq, 0).wait()
    weight_copy(wso, wo, 1).wait()
    weight_copy(wto, wo2, 2).wait()

    first_lane = pl.multiple_of(core * 512, 512)

    def place(h):
        low = core * 64 + h * HD
        return low, pl.multiple_of(jnp.minimum(low // 128, 3) * 128, 128)

    @pl.loop(0, 2)
    def _(f):
      @pl.when(f < count)
      def _():
        frame = i * 6 + jnp.where(f == 0, y, 4 + y // 2)
        lane96 = lax.broadcasted_iota(jnp.int32, (1, 96), 1)
        own_clip = jnp.sum(jnp.where(lane96 == frame, clip_row, 0), axis=1, keepdims=True)

        def own_mod(n):
            picked = jnp.zeros((1, D), F32)
            for c in range(4):
                picked = jnp.where(own_clip == c, mod[n, c : c + 1, :], picked)
            return picked

        shift, scale, gate = own_mod(0), own_mod(1), own_mod(2)

        @pl.loop(0, 4)
        def _(s):
            yy = (y + jnp.where(s == 0, 0, jnp.where(s == 1, 2, jnp.where(s == 2, 1, 3)))) % 4

            def arrived(block):
                pltpu.make_async_copy(tokens.at[0], xin.at[f, block], recv_a.at[f, block]).wait()

            arrived(yy * 2 + core)

            @pl.when(s > 0)
            def _():
                token_copy(xin.at[f, yy * 2 + core], f, yy * 2 + core, sibling).start()

            arrived(yy * 2 + 1 - core)
            rows = xin[f, pl.ds(2 * yy, 2)].astype(F32).reshape(256, D)
            hidden = normed(rows, shift, scale)
            at = pl.ds(pl.multiple_of(yy * 256, 256), 256)

            def project(n):
                return dot(hidden, wq[:, pl.ds(pl.multiple_of(n * D + first_lane, 128), WIDE)])

            q = (project(0) * Q_SCALE).reshape(2, 2, 2, 32, WIDE)
            for par in range(2):
                qtf[...] = q[:, :, par].reshape(128, WIDE).T
                cols = pl.ds(pl.multiple_of(par * 512 + yy * 128, 128), 128)
                for h in range(HALF):
                    low, off = place(h)
                    row = lax.broadcasted_iota(jnp.int32, (WIN, 1), 0) + (off - low)
                    inside = jnp.logical_and(row >= 0, row < HD)
                    qt_s[h, :, cols] = jnp.where(inside, qtf[pl.ds(off, WIN), :], 0.0).astype(BF16)
            k_s[at, :] = project(1).astype(BF16)
            vtf[...] = project(2).T
            for h in range(HALF):
                low, _ = place(h)
                vt_s[h, :HD, at] = vtf[pl.ds(pl.multiple_of(low, 8), HD), :].astype(BF16)

        @pl.when(f == count - 1)
        def _():
            weight_copy(wtq, wq, 3).start()

        @pl.loop(0, 2)
        def _(n):
            par = (x + n - core + 2) % 2
            cols = pl.ds(pl.multiple_of(par * 512, 512), 512)

            def scores(h, buf):
                _, off = place(h)
                score[buf] = dot(k_s[:, pl.ds(off, WIN)], qt_s[h, :, cols])

            def attend(h, buf):
                values = score[buf]
                top = jnp.max(values, axis=0, keepdims=True)
                power[buf] = jnp.exp2(values - top).astype(BF16)
                out = dot(vt_s[h], power[buf])
                mixt[pl.ds(pl.multiple_of(h * HD, 8), HD), :] = out[:HD] * (1.0 / out[HD : HD + 1])

            scores(0, 0)

            @pl.loop(0, HALF // 2)
            def _(u):
                scores(2 * u + 1, 1)
                attend(2 * u, 0)
                scores(jnp.minimum(2 * u + 2, HALF - 1), 0)
                attend(2 * u + 1, 1)

            own_rows = pl.ds(pl.multiple_of(core * HALF * HD, HALF * HD), HALF * HD)

            @pl.when(n == 0)
            def _():
                mix_out[f] = mixt[...].astype(BF16)
                pltpu.make_async_remote_copy(
                    src_ref=mix_out.at[f], dst_ref=mix_all.at[f, own_rows], send_sem=send_m, recv_sem=recv_m.at[f],
                    device_id=(i, sibling), device_id_type=MESH,
                ).start()

            @pl.when(n == 1)
            def _():
                mix_all[f, own_rows, :] = mixt[...].astype(BF16)
                pltpu.make_async_copy(mix_out.at[0], mix_out.at[0], recv_m.at[f]).wait()

                @pl.loop(0, 2)
                def _(b):
                    mixed = mix_all[f, :, pl.ds(pl.multiple_of(b * 256, 256), 256)].astype(F32).T.astype(BF16)
                    proj = dot(mixed, wo[...]).reshape(4, 2, 32, D)
                    devs = pl.ds(4 * b, 4)
                    for a in range(2):
                        at = pl.ds(pl.multiple_of(a * 64 + par * 32, 32), 32)
                        first = xin[f, devs, at, :].astype(F32) + gate * proj[:, a]
                        first_out[f, devs, a * 4 : a * 4 + 4] = first.reshape(4, 4, 8, D).astype(BF16)

                @pl.when(f == 0)
                def _():
                    pl.semaphore_wait(all_in, 7)

                slot = jnp.where(f == 0, i * 4 + y, 64 + i * 2 + y // 2)
                for dy, dz in YZ_FAR_FIRST:
                    for dc in range(2):
                        for k in range(2):
                            dx = (1 + core + 2 * k) % 4
                            to_x, to_z = (x + dx) % 4, (z + dz) % 4
                            dj = (y + dy) % 4 * 2 + (core + dc) % 2
                            src = first_out.at[f, dj, to_x // 2 * 4 + to_z]
                            copy = pltpu.make_async_remote_copy(
                                src_ref=src, dst_ref=recv_t.at[slot], send_sem=send_b,
                                recv_sem=recv_b.at[f], device_id=(to_x * 4 + to_z, dj), device_id_type=MESH,
                            )
                            if (dy, dz, dc, k) != (0, 0, 0, 1):
                                copy.start()
                            else:
                                pl.when(core == 0)(copy.start)

                @pl.when(core == 1)
                def _():
                    src = first_out.at[f, j, x // 2 * 4 + z]
                    pltpu.make_async_copy(src, recv_t.at[slot], recv_b.at[f]).start()

    weight_copy(wtq, wq, 3).wait()
    parts = ((0, 64, rows_a, qkv_a), (64, 32, rows_b, qkv_b))

    for f, (base, n, rows_f, qkv_f) in enumerate(parts):
        slots = recv_t.at[pl.ds(base, n)]
        pltpu.make_async_copy(slots, slots, recv_b.at[f]).wait()

        @pl.loop(0, n // 8)
        def _(c, base=base):
            rows = recv_t[pl.ds(base + c * 8, 8)].astype(F32).reshape(64, D)
            for b in range(9):
                f32_t[b, pl.ds(pl.multiple_of(base * 8 + c * 64, 64), 64), :] = rows[:, b * 128 : b * 128 + 128]

        @pl.loop(0, 8)
        def _(p, base=base, n=n, rows_f=rows_f):
            rows = jnp.concatenate([f32_t[b, pl.ds(base * 8 + p, n, stride=8), :] for b in range(9)], axis=1)
            at = pl.ds(pl.multiple_of(p * n, n), n)
            rows_f[at, :] = normed(rows, mods_t[0, base : base + n, :], mods_t[1, base : base + n, :])

        hidden = rows_f[...]
        qkv_f[:, :D] = (dot(hidden, wq[:, :D]) * Q_SCALE).astype(BF16)
        qkv_f[:, D : 2 * D] = dot(hidden, wq[:, D : 2 * D]).astype(BF16)
        qkv_f[:, 2 * D :] = dot(hidden, wq[:, 2 * D :]).astype(BF16)

    same = clip_col == clip_slots

    @pl.loop(0, 8)
    def _(p):
        at_a = pl.ds(pl.multiple_of(p * 64, 64), 64)
        at_b = pl.ds(pl.multiple_of(p * 32, 32), 32)
        blocks = [jnp.zeros((96, 128), F32) for _ in range(9)]
        for h in range(HEADS):
            off = window(h)
            lane = lax.broadcasted_iota(jnp.int32, (1, WIN), 1) + (off - h * HD)
            inside = jnp.logical_and(lane >= 0, lane < HD)

            def part(n):
                cols = slice(n * D + off, n * D + off + WIN)
                return jnp.concatenate([qkv_a[at_a, cols], qkv_b[at_b, cols]], axis=0)

            q = part(0)
            q = jnp.where(inside, q, jnp.zeros_like(q))
            scores = jnp.where(same, dot_t(q, part(1)), NEG)
            powers = jnp.exp2(scores - jnp.max(scores, axis=-1, keepdims=True))
            total = jnp.sum(powers, axis=-1, keepdims=True)
            out = dot(powers.astype(BF16), part(2)) * (1.0 / total)
            for b in range(off // 128, off // 128 + 2):
                lanes = slice(b * 128 - off, b * 128 - off + 128)
                blocks[b] = jnp.where(inside[:, lanes], out[:, lanes], blocks[b])
        for b in range(9):
            cols = slice(b * 128, b * 128 + 128)
            rows_a[at_a, cols] = blocks[b][:64].astype(BF16)
            rows_b[at_b, cols] = blocks[b][64:].astype(BF16)

    for f, (base, n, rows_f, _) in enumerate(parts):
        proj = dot(rows_f[...], wo2[...])
        for p in range(8):
            at = pl.ds(base * 8 + p, n, stride=8)
            for b in range(9):
                cols = slice(b * 128, b * 128 + 128)
                f32_t[b, at, :] = f32_t[b, at, :] + mods_t[2, base : base + n, cols] * proj[p * n : p * n + n, cols]

        @pl.loop(0, n // 8)
        def _(c, base=base):
            at = pl.ds(pl.multiple_of(base * 8 + c * 64, 64), 64)
            rows = jnp.concatenate([f32_t[b, at, :] for b in range(9)], axis=1)
            out_t[pl.ds(base + c * 8, 8)] = rows.reshape(8, 8, D).astype(BF16)

        size, start = (4, 0) if f == 0 else (2, 4)
        for dx, dz in XZ_FAR_FIRST:
            di = (x + dx) % 4 * 4 + (z + dz) % 4
            pltpu.make_async_remote_copy(
                src_ref=out_t.at[pl.ds(base + di * size, size)], dst_ref=final.at[pl.ds(start, size), i],
                send_sem=send_c, recv_sem=recv_c, device_id=(di, j), device_id_type=MESH,
            ).start()
        src = out_t.at[pl.ds(base + i * size, size)]
        pltpu.make_async_copy(src, final.at[pl.ds(start, size), i], recv_c).start()

    @pl.loop(0, 6 + 3 * count)
    def _(n):
        pltpu.make_async_copy(tokens.at[0], xin.at[0, 0], send_a).wait()

    @pl.loop(0, count)
    def _(n):
        pltpu.make_async_copy(mix_out.at[0], mix_out.at[0], send_m).wait()

    @pl.loop(0, count * (64 - core))
    def _(n):
        pltpu.make_async_copy(recv_t.at[0], recv_t.at[0], send_b).wait()

    @pl.loop(0, 15)
    def _(n):
        pltpu.make_async_copy(out_t.at[pl.ds(0, 6)], out_t.at[pl.ds(0, 6)], send_c).wait()

    pltpu.make_async_copy(final, final, recv_c).wait()


def body(tokens, clip_ids, modulation, w_spatial_qkv, w_spatial_out, w_temporal_qkv, w_temporal_out):
    any_, vmem = pl.BlockSpec(memory_space=pl.ANY), pl.BlockSpec(memory_space=pltpu.VMEM)
    dma = pltpu.SemaphoreType.DMA
    final = pl.pallas_call(
        kernel,
        out_shape=jax.ShapeDtypeStruct((6, 16, 8, D), BF16),
        in_specs=[any_, vmem, vmem, any_, any_, any_, any_],
        out_specs=any_,
        scratch_shapes=[
            pltpu.VMEM((2, 8, 128, D), BF16),
            pltpu.VMEM((D, 3 * D), BF16),
            pltpu.VMEM((D, D), BF16),
            pltpu.VMEM((D, D), BF16),
            pltpu.VMEM((WIDE, 128), F32),
            pltpu.VMEM((WIDE, 256), F32),
            pltpu.VMEM((HALF, WIN, 1024), BF16),
            pltpu.VMEM((1024, WIDE), BF16),
            pltpu.VMEM((HALF, HD + 8, 1024), BF16),
            pltpu.VMEM((2, 1024, 512), F32),
            pltpu.VMEM((2, 1024, 512), BF16),
            pltpu.VMEM((HALF * HD, 512), F32),
            pltpu.VMEM((2, HALF * HD, 512), BF16),
            pltpu.VMEM((2, D, 512), BF16),
            pltpu.VMEM((2, 8, 8, 8, D), BF16),
            pltpu.VMEM((96, 8, D), BF16),
            pltpu.VMEM((9, 768, 128), F32),
            pltpu.VMEM((512, D), BF16),
            pltpu.VMEM((256, D), BF16),
            pltpu.VMEM((512, 3 * D), BF16),
            pltpu.VMEM((256, 3 * D), BF16),
            pltpu.VMEM((96, 8, D), BF16),
            pltpu.VMEM((3, 96, D), F32),
            dma, dma((2, 8)), dma, dma((2,)), dma, dma((2,)), dma, dma, dma((4,)),
            pltpu.SemaphoreType.REGULAR,
        ],
        compiler_params=pltpu.CompilerParams(
            collective_id=0, has_side_effects=True, vmem_limit_bytes=63 * 1024 * 1024
        ),
        name="block",
    )(
        tokens, clip_ids.reshape(1, 96), modulation.transpose(1, 0, 2),
        w_spatial_qkv, w_spatial_out, w_temporal_qkv, w_temporal_out,
    )
    return final.reshape(6, 128, D)


def solution(mesh):
    in_specs = (P("frame", "inframe", None), P(), P(), P(), P(), P(), P())
    out_specs = P("frame", "inframe", None)
    return jax.shard_map(body, mesh=mesh, in_specs=in_specs, out_specs=out_specs, check_vma=False)
```

```python
import math

import jax
import jax.numpy as jnp
from jax import lax
from jax.experimental import pallas as pl
from jax.experimental.pallas import tpu as pltpu
from jax.sharding import PartitionSpec as P

MESH = pl.DeviceIdType.MESH
F32, BF16 = jnp.float32, jnp.bfloat16
HEADS = 16
HD = 72
D = HEADS * HD
WIN = 256
Q_SCALE = HD**-0.5 / math.log(2.0)
NEG = -1e30


def hops(*offsets):
    return sum(min(o, 4 - o) for o in offsets)


YZ_FAR_FIRST = sorted(((dy, dz) for dy in range(4) for dz in range(4)), key=lambda o: -hops(*o))
XZ_FAR_FIRST = YZ_FAR_FIRST[:-1]


def normed(x, shift, scale):
    center = x - jnp.mean(x, axis=-1, keepdims=True)
    spread = jnp.mean(center * center, axis=-1, keepdims=True)
    return (center * lax.rsqrt(spread + 1e-06) * (1.0 + scale) + shift).astype(BF16)


def dot(a, b):
    return jnp.dot(a, b, preferred_element_type=F32)


def dot_t(a, b):
    return lax.dot_general(a, b, (((1,), (1,)), ((), ())), preferred_element_type=F32)


def window(h):
    return min(h * HD // 128, 7) * 128


def kernel(
    tokens, clips, mod, wsq, wso, wtq, wto,
    final,
    xin, wq, wo, wo2, qtf, vtf, qt_s, k_s, vt_s, score, power, mixt, mix_out_0, mix_out_1, mix_0, mix_1,
    first_out, recv_t, f32_t,
    rows_a, rows_b, qkv_a, qkv_b, out_t, mods_t,
    send_a, recv_a, send_f, send_m, recv_m, send_b, recv_b, send_c, recv_c, w_sem, all_in,
):
    i = lax.axis_index("frame")
    j = lax.axis_index("inframe")
    x, z = i // 4, i % 4
    y, core = j // 2, j % 2
    sibling = y * 2 + 1 - core

    pair, member = y // 2, y % 2

    def weight_copy(src, dst, n):
        return pltpu.make_async_copy(src, dst, w_sem.at[n])

    barrier = pltpu.get_barrier_semaphore()

    @pl.loop(1, 8)
    def _(k):
        pl.semaphore_signal(barrier, inc=1, device_id=(i, (j + k) % 8), device_id_type=MESH)

    @pl.loop(1, 16)
    def _(k):
        pl.semaphore_signal(barrier, inc=1, device_id=((i + k) % 16, j), device_id_type=MESH)

    weight_copy(wsq, wq, 0).start()
    weight_copy(wso, wo, 1).start()
    weight_copy(wto, wo2, 2).start()
    pl.semaphore_wait(barrier, 22)

    def token_copy(src, f, block, dest):
        return pltpu.make_async_remote_copy(
            src_ref=src, dst_ref=xin.at[f, block], send_sem=send_a.at[f], recv_sem=recv_a.at[f, block],
            device_id=(i, dest), device_id_type=MESH,
        )

    def send_tokens(f):
        def owned(chip):
            return chip if f == 0 else 4 + chip // 2

        for dy in (2, 1, 3):
            chip = (y + dy) % 4
            token_copy(tokens.at[owned(chip)], f, j, chip * 2 + core).start()
        token_copy(tokens.at[owned(y)], f, j, sibling).start()
        pltpu.make_async_copy(tokens.at[owned(y)], xin.at[f, j], recv_a.at[f, j]).start()

    send_tokens(0)

    @pl.loop(1, 8)
    def _(k):
        pl.semaphore_signal(all_in, inc=1, device_id=(i, (j + k) % 8), device_id_type=MESH)

    def frame_at(slot):
        late = slot - 64
        return jnp.where(slot < 64, slot // 4 * 6 + slot % 4, late // 2 * 6 + 4 + late % 2)

    clip_row = clips[...]
    row_id = lax.broadcasted_iota(jnp.int32, (96, 96), 0)
    col_id = lax.broadcasted_iota(jnp.int32, (96, 96), 1)
    clip_rows = jnp.broadcast_to(clip_row, (96, 96))
    clip_natural = jnp.sum(jnp.where(row_id == col_id, clip_rows, 0), axis=1, keepdims=True)
    clip_col = jnp.sum(jnp.where(frame_at(row_id) == col_id, clip_rows, 0), axis=1, keepdims=True)
    clip_slots = jnp.sum(jnp.where(row_id == frame_at(col_id), clip_natural, 0), axis=0, keepdims=True)

    @pl.loop(0, 3)
    def _(n):
        picked = jnp.zeros((96, D), F32)
        for c in range(4):
            picked = jnp.where(clip_col == c, mod[3 + n, c : c + 1, :], picked)
        mods_t[n] = picked

    vt_s[:, HD:, :] = jnp.ones((HEADS // 2, 8, 1024), BF16)

    weight_copy(wsq, wq, 0).wait()
    weight_copy(wso, wo, 1).wait()
    weight_copy(wto, wo2, 2).wait()

    def spatial(f):
        heads, wide = (8, 640) if f == 0 else (4, 384)
        share = core if f == 0 else member * 2 + core
        features = heads * HD
        lane_gap = 512 if f == 0 else 256
        first_lane = pl.multiple_of(share * lane_gap, 256)
        frame = i * 6 + (y if f == 0 else 4 + pair)
        own_clip = jnp.sum(jnp.where(lane96 == frame, clip_row, 0), axis=1, keepdims=True)

        def own_mod(n):
            picked = jnp.zeros((1, D), F32)
            for c in range(4):
                picked = jnp.where(own_clip == c, mod[n, c : c + 1, :], picked)
            return picked

        shift, scale, gate = own_mod(0), own_mod(1), own_mod(2)

        def place(h):
            low = share * (features - lane_gap) + h * HD
            return low, pl.multiple_of(jnp.minimum(low // 128, wide // 128 - 2) * 128, 128)

        @pl.loop(0, 4)
        def _(s):
            yy = (y + jnp.where(s == 0, 0, jnp.where(s == 1, 2, jnp.where(s == 2, 1, 3)))) % 4

            if f == 0:
                @pl.when(s == 1)
                def _():
                    for _ in range(4):
                        pltpu.make_async_copy(tokens.at[0], xin.at[0, 0], send_a.at[0]).wait()
                    send_tokens(1)

            def arrived(block):
                pltpu.make_async_copy(tokens.at[0], xin.at[f, block], recv_a.at[f, block]).wait()

            arrived(yy * 2 + core)

            @pl.when(s > 0)
            def _():
                pltpu.make_async_remote_copy(
                    src_ref=xin.at[f, yy * 2 + core], dst_ref=xin.at[f, yy * 2 + core], send_sem=send_f,
                    recv_sem=recv_a.at[f, yy * 2 + core], device_id=(i, sibling), device_id_type=MESH,
                ).start()

            arrived(yy * 2 + 1 - core)
            rows = xin[f, pl.ds(2 * yy, 2)].astype(F32).reshape(256, D)
            hidden = normed(rows, shift, scale)
            at = pl.ds(pl.multiple_of(yy * 256, 256), 256)

            def project(n):
                return dot(hidden, wq[:, pl.ds(pl.multiple_of(n * D + first_lane, 128), wide)])

            q = (project(0) * Q_SCALE).reshape(2, 2, 2, 32, wide)
            for par in range(2):
                qtf[:wide] = q[:, :, par].reshape(128, wide).T
                cols = pl.ds(pl.multiple_of(par * 512 + yy * 128, 128), 128)
                for h in range(heads):
                    low, off = place(h)
                    row = lax.broadcasted_iota(jnp.int32, (WIN, 1), 0) + (off - low)
                    inside = jnp.logical_and(row >= 0, row < HD)
                    qt_s[h, :, cols] = jnp.where(inside, qtf[pl.ds(off, WIN), :], 0.0).astype(BF16)
            k_s[at, :wide] = project(1).astype(BF16)
            vtf[:wide] = project(2).T
            for h in range(heads):
                low, _ = place(h)
                vt_s[h, :HD, at] = vtf[pl.ds(pl.multiple_of(low, 8), HD), :].astype(BF16)

        if f == 1:
            weight_copy(wtq, wq, 3).start()

        own_rows = pl.ds(pl.multiple_of(share * features, features), features)
        mix_f = mix_0 if f == 0 else mix_1

        def hand_over(src, dest):
            pltpu.make_async_remote_copy(
                src_ref=src, dst_ref=mix_f.at[own_rows], send_sem=send_m.at[f], recv_sem=recv_m.at[f],
                device_id=(i, dest), device_id_type=MESH,
            ).start()

        @pl.loop(0, 2)
        def _(n):
            par = (x + n - core + 2) % 2
            cols = pl.ds(pl.multiple_of(par * 512, 512), 512)

            def scores(h, buf):
                _, off = place(h)
                score[buf] = dot(k_s[:, pl.ds(off, WIN)], qt_s[h, :, cols])

            def attend(h, buf):
                values = score[buf]
                top = jnp.max(values, axis=0, keepdims=True)
                power[buf] = jnp.exp2(values - top).astype(BF16)
                out = dot(vt_s[h], power[buf])
                mixt[pl.ds(pl.multiple_of(h * HD, 8), HD), :] = out[:HD] * (1.0 / out[HD : HD + 1])

            scores(0, 0)

            @pl.loop(0, heads // 2)
            def _(u):
                scores(2 * u + 1, 1)
                attend(2 * u, 0)
                scores(jnp.minimum(2 * u + 2, heads - 1), 0)
                attend(2 * u + 1, 1)

            if f == 0:
                @pl.when(n == 0)
                def _():
                    mix_out_0[...] = mixt[...].astype(BF16)
                    hand_over(mix_out_0, sibling)

                @pl.when(n == 1)
                def _():
                    mix_0[own_rows, :] = mixt[...].astype(BF16)
            else:
                there = y + 1 - 2 * member

                @pl.when(n == 0)
                def _():
                    for b in range(2):
                        mix_out_1[b] = mixt[:features, b * 256 : b * 256 + 256].astype(BF16)
                        hand_over(mix_out_1.at[b], (pair * 2 + b) * 2 + 1 - core)

                @pl.when(n == 1)
                def _():
                    for b in range(2):
                        part = mixt[:features, b * 256 : b * 256 + 256].astype(BF16)

                        @pl.when(member == b)
                        def _(part=part):
                            mix_1[own_rows, :] = part

                        @pl.when(member != b)
                        def _(part=part):
                            mix_out_1[2] = part
                            hand_over(mix_out_1.at[2], there * 2 + core)

        arriving = mix_out_0 if f == 0 else mix_out_1
        pltpu.make_async_copy(arriving, arriving, recv_m.at[f]).wait()
        par = (x + core + 1) % 2

        def finish(b, mixed):
            proj = dot(mixed.astype(F32).T.astype(BF16), wo[...]).reshape(4, 2, 32, D)
            devs = pl.ds(4 * b, 4)
            for a in range(2):
                at = pl.ds(pl.multiple_of(a * 64 + par * 32, 32), 32)
                first = xin[f, devs, at, :].astype(F32) + gate * proj[:, a]
                first_out[f, devs, a * 4 : a * 4 + 4] = first.reshape(4, 4, 8, D).astype(BF16)

        if f == 0:
            @pl.loop(0, 2)
            def _(b):
                finish(b, mix_0[:, pl.ds(pl.multiple_of(b * 256, 256), 256)])

            pl.semaphore_wait(all_in, 7)
            to_chips = [((y + dy) % 4, dy == 0) for dy in (2, 1, 3, 0)]
        else:
            finish(member, mix_1[...])
            to_chips = [(member * 2, None), (member * 2 + 1, None)]

        slot = i * 4 + y if f == 0 else 64 + i * 2 + pair
        for dz in (2, 1, 3, 0):
            for chip, same_chip in to_chips:
                for dc in range(2):
                    for k in range(2):
                        to_x, to_z = (x + 1 + core + 2 * k) % 4, (z + dz) % 4
                        dj = chip * 2 + (core + dc) % 2
                        src = first_out.at[f, dj, to_x // 2 * 4 + to_z]
                        copy = pltpu.make_async_remote_copy(
                            src_ref=src, dst_ref=recv_t.at[slot], send_sem=send_b.at[f],
                            recv_sem=recv_b.at[f], device_id=(to_x * 4 + to_z, dj), device_id_type=MESH,
                        )
                        if dz or dc or k == 0 or same_chip is False:
                            copy.start()
                        else:
                            here = jnp.logical_and(core == 1, chip == y)
                            pl.when(jnp.logical_not(here))(copy.start)
                            pl.when(here)(pltpu.make_async_copy(src, recv_t.at[slot], recv_b.at[f]).start)

    lane96 = lax.broadcasted_iota(jnp.int32, (1, 96), 1)
    spatial(0)
    spatial(1)

    weight_copy(wtq, wq, 3).wait()
    parts = ((0, 64, rows_a, qkv_a), (64, 32, rows_b, qkv_b))

    for f, (base, n, rows_f, qkv_f) in enumerate(parts):
        slots = recv_t.at[pl.ds(base, n)]
        pltpu.make_async_copy(slots, slots, recv_b.at[f]).wait()

        @pl.loop(0, n // 8)
        def _(c, base=base):
            rows = recv_t[pl.ds(base + c * 8, 8)].astype(F32).reshape(64, D)
            for b in range(9):
                f32_t[b, pl.ds(pl.multiple_of(base * 8 + c * 64, 64), 64), :] = rows[:, b * 128 : b * 128 + 128]

        @pl.loop(0, 8)
        def _(p, base=base, n=n, rows_f=rows_f):
            rows = jnp.concatenate([f32_t[b, pl.ds(base * 8 + p, n, stride=8), :] for b in range(9)], axis=1)
            at = pl.ds(pl.multiple_of(p * n, n), n)
            rows_f[at, :] = normed(rows, mods_t[0, base : base + n, :], mods_t[1, base : base + n, :])

        hidden = rows_f[...]
        qkv_f[:, :D] = (dot(hidden, wq[:, :D]) * Q_SCALE).astype(BF16)
        qkv_f[:, D : 2 * D] = dot(hidden, wq[:, D : 2 * D]).astype(BF16)
        qkv_f[:, 2 * D :] = dot(hidden, wq[:, 2 * D :]).astype(BF16)

    same = clip_col == clip_slots

    for f, (base, n, rows_f, qkv_f) in enumerate(parts):
        @pl.loop(0, 8)
        def _(p, base=base, n=n, rows_f=rows_f, qkv_f=qkv_f):
            at = pl.ds(pl.multiple_of(p * n, n), n)
            at_a = pl.ds(pl.multiple_of(p * 64, 64), 64)
            at_b = pl.ds(pl.multiple_of(p * 32, 32), 32)
            blocks = [jnp.zeros((n, 128), F32) for _ in range(9)]
            for h in range(HEADS):
                off = window(h)
                lane = lax.broadcasted_iota(jnp.int32, (1, WIN), 1) + (off - h * HD)
                inside = jnp.logical_and(lane >= 0, lane < HD)

                def part(m):
                    cols = slice(m * D + off, m * D + off + WIN)
                    return jnp.concatenate([qkv_a[at_a, cols], qkv_b[at_b, cols]], axis=0)

                q = qkv_f[at, off : off + WIN]
                q = jnp.where(inside, q, jnp.zeros_like(q))
                scores = jnp.where(same[base : base + n], dot_t(q, part(1)), NEG)
                powers = jnp.exp2(scores - jnp.max(scores, axis=-1, keepdims=True))
                total = jnp.sum(powers, axis=-1, keepdims=True)
                out = dot(powers.astype(BF16), part(2)) * (1.0 / total)
                for b in range(off // 128, off // 128 + 2):
                    lanes = slice(b * 128 - off, b * 128 - off + 128)
                    blocks[b] = jnp.where(inside[:, lanes], out[:, lanes], blocks[b])
            for b in range(9):
                rows_f[at, b * 128 : b * 128 + 128] = blocks[b].astype(BF16)

        proj = dot(rows_f[...], wo2[...])
        for p in range(8):
            at = pl.ds(base * 8 + p, n, stride=8)
            for b in range(9):
                cols = slice(b * 128, b * 128 + 128)
                f32_t[b, at, :] = f32_t[b, at, :] + mods_t[2, base : base + n, cols] * proj[p * n : p * n + n, cols]

        @pl.loop(0, n // 8)
        def _(c, base=base):
            at = pl.ds(pl.multiple_of(base * 8 + c * 64, 64), 64)
            rows = jnp.concatenate([f32_t[b, at, :] for b in range(9)], axis=1)
            out_t[pl.ds(base + c * 8, 8)] = rows.reshape(8, 8, D).astype(BF16)

        size, start = (4, 0) if f == 0 else (2, 4)
        for dx, dz in XZ_FAR_FIRST:
            di = (x + dx) % 4 * 4 + (z + dz) % 4
            pltpu.make_async_remote_copy(
                src_ref=out_t.at[pl.ds(base + di * size, size)], dst_ref=final.at[pl.ds(start, size), i],
                send_sem=send_c, recv_sem=recv_c, device_id=(di, j), device_id_type=MESH,
            ).start()
        src = out_t.at[pl.ds(base + i * size, size)]
        pltpu.make_async_copy(src, final.at[pl.ds(start, size), i], recv_c).start()

    for _ in range(4):
        pltpu.make_async_copy(tokens.at[0], xin.at[0, 0], send_a.at[1]).wait()
    for _ in range(6):
        pltpu.make_async_copy(tokens.at[0], xin.at[0, 0], send_f).wait()
    pltpu.make_async_copy(mix_out_0, mix_out_0, send_m.at[0]).wait()
    for _ in range(3):
        pltpu.make_async_copy(mix_out_1.at[0], mix_out_1.at[0], send_m.at[1]).wait()

    @pl.loop(0, 64 - core)
    def _(n):
        pltpu.make_async_copy(recv_t.at[0], recv_t.at[0], send_b.at[0]).wait()

    self_sent = jnp.where(jnp.logical_and(core == 1, pair == member), 1, 0)

    @pl.loop(0, 32 - self_sent)
    def _(n):
        pltpu.make_async_copy(recv_t.at[0], recv_t.at[0], send_b.at[1]).wait()

    @pl.loop(0, 15)
    def _(n):
        pltpu.make_async_copy(out_t.at[pl.ds(0, 6)], out_t.at[pl.ds(0, 6)], send_c).wait()

    pltpu.make_async_copy(final, final, recv_c).wait()


def body(tokens, clip_ids, modulation, w_spatial_qkv, w_spatial_out, w_temporal_qkv, w_temporal_out):
    any_, vmem = pl.BlockSpec(memory_space=pl.ANY), pl.BlockSpec(memory_space=pltpu.VMEM)
    dma = pltpu.SemaphoreType.DMA
    final = pl.pallas_call(
        kernel,
        out_shape=jax.ShapeDtypeStruct((6, 16, 8, D), BF16),
        in_specs=[any_, vmem, vmem, any_, any_, any_, any_],
        out_specs=any_,
        scratch_shapes=[
            pltpu.VMEM((2, 8, 128, D), BF16),
            pltpu.VMEM((D, 3 * D), BF16),
            pltpu.VMEM((D, D), BF16),
            pltpu.VMEM((D, D), BF16),
            pltpu.VMEM((640, 128), F32),
            pltpu.VMEM((640, 256), F32),
            pltpu.VMEM((HEADS // 2, WIN, 1024), BF16),
            pltpu.VMEM((1024, 640), BF16),
            pltpu.VMEM((HEADS // 2, HD + 8, 1024), BF16),
            pltpu.VMEM((2, 1024, 512), F32),
            pltpu.VMEM((2, 1024, 512), BF16),
            pltpu.VMEM((D // 2, 512), F32),
            pltpu.VMEM((D // 2, 512), BF16),
            pltpu.VMEM((3, D // 4, 256), BF16),
            pltpu.VMEM((D, 512), BF16),
            pltpu.VMEM((D, 256), BF16),
            pltpu.VMEM((2, 8, 8, 8, D), BF16),
            pltpu.VMEM((96, 8, D), BF16),
            pltpu.VMEM((9, 768, 128), F32),
            pltpu.VMEM((512, D), BF16),
            pltpu.VMEM((256, D), BF16),
            pltpu.VMEM((512, 3 * D), BF16),
            pltpu.VMEM((256, 3 * D), BF16),
            pltpu.VMEM((96, 8, D), BF16),
            pltpu.VMEM((3, 96, D), F32),
            dma((2,)), dma((2, 8)), dma, dma((2,)), dma((2,)), dma((2,)), dma((2,)), dma, dma, dma((4,)),
            pltpu.SemaphoreType.REGULAR,
        ],
        compiler_params=pltpu.CompilerParams(
            collective_id=0, has_side_effects=True, vmem_limit_bytes=63 * 1024 * 1024
        ),
        name="block",
    )(
        tokens, clip_ids.reshape(1, 96), modulation.transpose(1, 0, 2),
        w_spatial_qkv, w_spatial_out, w_temporal_qkv, w_temporal_out,
    )
    return final.reshape(6, 128, D)


def solution(mesh):
    in_specs = (P("frame", "inframe", None), P(), P(), P(), P(), P(), P())
    out_specs = P("frame", "inframe", None)
    return jax.shard_map(body, mesh=mesh, in_specs=in_specs, out_specs=out_specs, check_vma=False)
```

```python
import math

import jax
import jax.numpy as jnp
from jax import lax
from jax.experimental import pallas as pl
from jax.experimental.pallas import tpu as pltpu
from jax.sharding import PartitionSpec as P

MESH = pl.DeviceIdType.MESH
F32, BF16 = jnp.float32, jnp.bfloat16
HEADS = 16
HD = 72
D = HEADS * HD
WIN = 256
Q_SCALE = HD**-0.5 / math.log(2.0)
NEG = -1e30


YZ_FAR_FIRST = [(2, 2), (1, 2), (2, 1), (3, 2), (2, 3), (1, 1), (3, 3), (1, 3), (3, 1), (2, 0), (0, 2)]
YZ_FAR_FIRST += [(1, 0), (0, 1), (3, 0), (0, 3), (0, 0)]
XZ_FAR_FIRST = YZ_FAR_FIRST[:-1]


def normed(x, shift, scale):
    center = x - jnp.mean(x, axis=-1, keepdims=True)
    spread = jnp.mean(center * center, axis=-1, keepdims=True)
    return (center * lax.rsqrt(spread + 1e-06) * (1.0 + scale) + shift).astype(BF16)


def dot(a, b):
    return jnp.dot(a, b, preferred_element_type=F32)


def dot_t(a, b):
    return lax.dot_general(a, b, (((1,), (1,)), ((), ())), preferred_element_type=F32)


def window(h):
    return min(h * HD // 128, 7) * 128


def kernel(
    tokens, clips, mod, wsq, wso, wtq, wto,
    final,
    xin, wq, ws, wo, wo2, qtf, vtf, qt_s, k_s, vt_s, score, power, mixt, mix_out_0, mix_out_1, mix_0, mix_1,
    first_out, recv_t, f32_t,
    rows_a, rows_b, qkv_a, qkv_b, mods_t,
    send_a, recv_a, send_f, send_m, recv_m, send_b, recv_b, send_c, recv_c, w_sem, all_in,
):
    i = lax.axis_index("frame")
    j = lax.axis_index("inframe")
    x, z = i // 4, i % 4
    y, core = j // 2, j % 2
    sibling = y * 2 + 1 - core

    pair, member = y // 2, y % 2

    def weight_copy(src, dst, n):
        return pltpu.make_async_copy(src, dst, w_sem.at[n])

    barrier = pltpu.get_barrier_semaphore()

    @pl.loop(1, 8)
    def _(k):
        pl.semaphore_signal(barrier, inc=1, device_id=(i, (j + k) % 8), device_id_type=MESH)

    @pl.loop(1, 16)
    def _(k):
        pl.semaphore_signal(barrier, inc=1, device_id=((i + k) % 16, j), device_id_type=MESH)

    def head_columns(f):
        wide, lane_gap = (640, 512) if f == 0 else (384, 256)
        share = core if f == 0 else member * 2 + core
        return [
            weight_copy(
                wsq.at[:, pl.ds(pl.multiple_of(n * D + share * lane_gap, 128), wide)],
                ws.at[:, n * wide : n * wide + wide], 3 * f + n,
            )
            for n in range(3)
        ]

    for copy in head_columns(0):
        copy.start()
    weight_copy(wso, wo, 6).start()
    weight_copy(wto, wo2, 7).start()
    weight_copy(wtq, wq, 8).start()
    pl.semaphore_wait(barrier, 22)

    def token_copy(src, f, block, dest):
        return pltpu.make_async_remote_copy(
            src_ref=src, dst_ref=xin.at[f, block], send_sem=send_a.at[f], recv_sem=recv_a.at[f, block],
            device_id=(i, dest), device_id_type=MESH,
        )

    def send_tokens(f):
        def owned(chip):
            return chip if f == 0 else 4 + chip // 2

        for dy in (2, 1, 3):
            chip = (y + dy) % 4
            token_copy(tokens.at[owned(chip)], f, j, chip * 2 + core).start()
        token_copy(tokens.at[owned(y)], f, j, sibling).start()
        pltpu.make_async_copy(tokens.at[owned(y)], xin.at[f, j], recv_a.at[f, j]).start()

    send_tokens(0)

    @pl.loop(1, 8)
    def _(k):
        pl.semaphore_signal(all_in, inc=1, device_id=(i, (j + k) % 8), device_id_type=MESH)

    def frame_at(slot):
        late = slot - 64
        return jnp.where(slot < 64, slot // 4 * 6 + slot % 4, late // 2 * 6 + 4 + late % 2)

    clip_row = clips[...]
    row_id = lax.broadcasted_iota(jnp.int32, (96, 96), 0)
    col_id = lax.broadcasted_iota(jnp.int32, (96, 96), 1)
    clip_rows = jnp.broadcast_to(clip_row, (96, 96))
    clip_natural = jnp.sum(jnp.where(row_id == col_id, clip_rows, 0), axis=1, keepdims=True)
    clip_col = jnp.sum(jnp.where(frame_at(row_id) == col_id, clip_rows, 0), axis=1, keepdims=True)
    clip_slots = jnp.sum(jnp.where(row_id == frame_at(col_id), clip_natural, 0), axis=0, keepdims=True)

    @pl.loop(0, 3)
    def _(n):
        picked = jnp.zeros((96, D), F32)
        for c in range(4):
            picked = jnp.where(clip_col == c, mod[3 + n, c : c + 1, :], picked)
        mods_t[n] = picked

    vt_s[:, HD:, :] = jnp.ones((HEADS // 2, 8, 1024), BF16)

    for copy in head_columns(0):
        copy.wait()
    weight_copy(wso, wo, 6).wait()
    weight_copy(wto, wo2, 7).wait()
    weight_copy(wtq, wq, 8).wait()

    def arrived(f, block):
        pltpu.make_async_copy(tokens.at[0], xin.at[f, block], recv_a.at[f, block]).wait()

    def forward(f):
        for dy in (2, 1, 3):
            block = (y + dy) % 4 * 2 + core
            arrived(f, block)
            pltpu.make_async_remote_copy(
                src_ref=xin.at[f, block], dst_ref=xin.at[f, block], send_sem=send_f,
                recv_sem=recv_a.at[f, block], device_id=(i, sibling), device_id_type=MESH,
            ).start()

    def spatial(f):
        heads, wide = (8, 640) if f == 0 else (4, 384)
        share = core if f == 0 else member * 2 + core
        features = heads * HD
        lane_gap = 512 if f == 0 else 256
        frame = i * 6 + (y if f == 0 else 4 + pair)
        own_clip = jnp.sum(jnp.where(lane96 == frame, clip_row, 0), axis=1, keepdims=True)

        def own_mod(n):
            picked = jnp.zeros((1, D), F32)
            for c in range(4):
                picked = jnp.where(own_clip == c, mod[n, c : c + 1, :], picked)
            return picked

        shift, scale, gate = own_mod(0), own_mod(1), own_mod(2)

        def place(h):
            low = share * (features - lane_gap) + h * HD
            return low, pl.multiple_of(jnp.minimum(low // 128, wide // 128 - 2) * 128, 128)

        arrived(f, j)
        if f == 1:
            for copy in head_columns(1):
                copy.wait()

        @pl.loop(0, 4)
        def _(s):
            yy = (y + jnp.where(s == 0, 0, jnp.where(s == 1, 2, jnp.where(s == 2, 1, 3)))) % 4

            if f == 0:
                @pl.when(s == 1)
                def _():
                    for _ in range(4):
                        pltpu.make_async_copy(tokens.at[0], xin.at[0, 0], send_a.at[0]).wait()
                    send_tokens(1)
                    forward(0)

            arrived(f, yy * 2 + 1 - core)
            rows = xin[f, pl.ds(2 * yy, 2)].astype(F32).reshape(256, D)
            hidden = normed(rows, shift, scale)
            at = pl.ds(pl.multiple_of(yy * 256, 256), 256)

            qkv = dot(hidden, ws[:, : 3 * wide])
            q = (qkv[:, :wide] * Q_SCALE).reshape(2, 2, 2, 32, wide)
            for par in range(2):
                qtf[:wide] = q[:, :, par].reshape(128, wide).T
                cols = pl.ds(pl.multiple_of(par * 512 + yy * 128, 128), 128)
                for h in range(heads):
                    low, off = place(h)
                    row = lax.broadcasted_iota(jnp.int32, (WIN, 1), 0) + (off - low)
                    inside = jnp.logical_and(row >= 0, row < HD)
                    qt_s[h, :, cols] = jnp.where(inside, qtf[pl.ds(off, WIN), :], 0.0).astype(BF16)
            k_s[at, :wide] = qkv[:, wide : 2 * wide].astype(BF16)
            vtf[:wide] = qkv[:, 2 * wide :].T
            for h in range(heads):
                low, _ = place(h)
                vt_s[h, :HD, at] = vtf[pl.ds(pl.multiple_of(low, 8), HD), :].astype(BF16)

        if f == 0:
            for copy in head_columns(1):
                copy.start()

        own_rows = pl.ds(pl.multiple_of(share * features, features), features)
        mix_f = mix_0 if f == 0 else mix_1

        def hand_over(src, dest):
            pltpu.make_async_remote_copy(
                src_ref=src, dst_ref=mix_f.at[own_rows], send_sem=send_m.at[f], recv_sem=recv_m.at[f],
                device_id=(i, dest), device_id_type=MESH,
            ).start()

        @pl.loop(0, 2)
        def _(n):
            par = (x + n - core + 2) % 2
            cols = pl.ds(pl.multiple_of(par * 512, 512), 512)

            def scores(h, buf):
                _, off = place(h)
                score[buf] = dot(k_s[:, pl.ds(off, WIN)], qt_s[h, :, cols])

            def attend(h, buf):
                values = score[buf]
                top = jnp.max(values, axis=0, keepdims=True)
                power[buf] = jnp.exp2(values - top).astype(BF16)
                out = dot(vt_s[h], power[buf])
                mixt[pl.ds(pl.multiple_of(h * HD, 8), HD), :] = out[:HD] * (1.0 / out[HD : HD + 1])

            scores(0, 0)

            @pl.loop(0, heads // 2)
            def _(u):
                scores(2 * u + 1, 1)
                attend(2 * u, 0)
                scores(jnp.minimum(2 * u + 2, heads - 1), 0)
                attend(2 * u + 1, 1)

            if f == 0:
                @pl.when(n == 0)
                def _():
                    mix_out_0[...] = mixt[...].astype(BF16)
                    hand_over(mix_out_0, sibling)

                @pl.when(n == 1)
                def _():
                    mix_0[own_rows, :] = mixt[...].astype(BF16)
            else:
                there = y + 1 - 2 * member

                @pl.when(n == 0)
                def _():
                    for b in range(2):
                        mix_out_1[b] = mixt[:features, b * 256 : b * 256 + 256].astype(BF16)
                        hand_over(mix_out_1.at[b], (pair * 2 + b) * 2 + 1 - core)

                @pl.when(n == 1)
                def _():
                    for b in range(2):
                        part = mixt[:features, b * 256 : b * 256 + 256].astype(BF16)

                        @pl.when(member == b)
                        def _(part=part):
                            mix_1[own_rows, :] = part

                        @pl.when(member != b)
                        def _(part=part):
                            mix_out_1[2] = part
                            hand_over(mix_out_1.at[2], there * 2 + core)

        if f == 0:
            forward(1)
        arriving = mix_out_0 if f == 0 else mix_out_1
        pltpu.make_async_copy(arriving, arriving, recv_m.at[f]).wait()
        par = (x + core + 1) % 2

        def finish(b, mixed):
            proj = dot(mixed.astype(F32).T.astype(BF16), wo[...]).reshape(4, 2, 32, D)
            devs = pl.ds(4 * b, 4)
            for a in range(2):
                at = pl.ds(pl.multiple_of(a * 64 + par * 32, 32), 32)
                first = xin[f, devs, at, :].astype(F32) + gate * proj[:, a]
                first_out[f, devs, a * 4 : a * 4 + 4] = first.reshape(4, 4, 8, D).astype(BF16)

        if f == 0:
            @pl.loop(0, 2)
            def _(b):
                finish(b, mix_0[:, pl.ds(pl.multiple_of(b * 256, 256), 256)])

            pl.semaphore_wait(all_in, 7)
            targets = [((y + dy) % 4, dz, dy == 0) for dy, dz in YZ_FAR_FIRST]
        else:
            finish(member, mix_1[...])
            targets = [(member * 2 + e, dz, True) for dz in (2, 1, 3, 0) for e in range(2)]

        slot = i * 4 + y if f == 0 else 64 + i * 2 + pair
        for chip, dz, may_be_here in targets:
            for k in range(2):
                for dc in range(2):
                    to_x, to_z = (x + 1 + core + 2 * k) % 4, (z + dz) % 4
                    dj = chip * 2 + (core + dc) % 2
                    src = first_out.at[f, dj, to_x // 2 * 4 + to_z]
                    copy = pltpu.make_async_remote_copy(
                        src_ref=src, dst_ref=recv_t.at[slot], send_sem=send_b.at[f],
                        recv_sem=recv_b.at[f], device_id=(to_x * 4 + to_z, dj), device_id_type=MESH,
                    )
                    if dz or dc or k == 0 or not may_be_here:
                        copy.start()
                    else:
                        here = jnp.logical_and(core == 1, chip == y)
                        pl.when(jnp.logical_not(here))(copy.start)
                        pl.when(here)(pltpu.make_async_copy(src, recv_t.at[slot], recv_b.at[f]).start)

    lane96 = lax.broadcasted_iota(jnp.int32, (1, 96), 1)
    spatial(0)
    spatial(1)

    parts = ((0, 64, rows_a, qkv_a), (64, 32, rows_b, qkv_b))

    for f, (base, n, rows_f, qkv_f) in enumerate(parts):
        slots = recv_t.at[pl.ds(base, n)]
        pltpu.make_async_copy(slots, slots, recv_b.at[f]).wait()

        @pl.loop(0, n // 8)
        def _(c, base=base):
            rows = recv_t[pl.ds(base + c * 8, 8)].astype(F32).reshape(64, D)
            for b in range(9):
                f32_t[b, pl.ds(pl.multiple_of(base * 8 + c * 64, 64), 64), :] = rows[:, b * 128 : b * 128 + 128]

        @pl.loop(0, 8)
        def _(p, base=base, n=n, rows_f=rows_f):
            rows = jnp.concatenate([f32_t[b, pl.ds(base * 8 + p, n, stride=8), :] for b in range(9)], axis=1)
            at = pl.ds(pl.multiple_of(p * n, n), n)
            rows_f[at, :] = normed(rows, mods_t[0, base : base + n, :], mods_t[1, base : base + n, :])

        hidden = rows_f[...]
        qkv_f[:, :D] = (dot(hidden, wq[:, :D]) * Q_SCALE).astype(BF16)
        qkv_f[:, D:] = dot(hidden, wq[:, D:]).astype(BF16)

    same = clip_col == clip_slots

    def attend_position(p):
        at_a = pl.ds(pl.multiple_of(p * 64, 64), 64)
        at_b = pl.ds(pl.multiple_of(p * 32, 32), 32)
        blocks = [jnp.zeros((96, 128), F32) for _ in range(9)]
        for h in range(HEADS):
            off = window(h)
            lane = lax.broadcasted_iota(jnp.int32, (1, WIN), 1) + (off - h * HD)
            inside = jnp.logical_and(lane >= 0, lane < HD)

            def part(m):
                cols = slice(m * D + off, m * D + off + WIN)
                return jnp.concatenate([qkv_a[at_a, cols], qkv_b[at_b, cols]], axis=0)

            q = part(0)
            q = jnp.where(inside, q, jnp.zeros_like(q))
            scores = jnp.where(same, dot_t(q, part(1)), NEG)
            powers = jnp.exp2(scores - jnp.max(scores, axis=-1, keepdims=True))
            total = jnp.sum(powers, axis=-1, keepdims=True)
            out = dot(powers.astype(BF16), part(2)) * (1.0 / total)
            for b in range(off // 128, off // 128 + 2):
                lanes = slice(b * 128 - off, b * 128 - off + 128)
                blocks[b] = jnp.where(inside[:, lanes], out[:, lanes], blocks[b])
        for b in range(9):
            cols = slice(b * 128, b * 128 + 128)
            rows_a[at_a, cols] = blocks[b][:64].astype(BF16)
            rows_b[at_b, cols] = blocks[b][64:].astype(BF16)

    @pl.loop(0, 4)
    def _(u):
        attend_position(2 * u)
        attend_position(2 * u + 1)

    for f, (base, n, rows_f, _) in enumerate(parts):
        proj = dot(rows_f[...], wo2[...])
        for p in range(8):
            at = pl.ds(base * 8 + p, n, stride=8)
            for b in range(9):
                cols = slice(b * 128, b * 128 + 128)
                f32_t[b, at, :] = f32_t[b, at, :] + mods_t[2, base : base + n, cols] * proj[p * n : p * n + n, cols]

        @pl.loop(0, n // 8)
        def _(c, base=base):
            at = pl.ds(pl.multiple_of(base * 8 + c * 64, 64), 64)
            rows = jnp.concatenate([f32_t[b, at, :] for b in range(9)], axis=1)
            recv_t[pl.ds(base + c * 8, 8)] = rows.reshape(8, 8, D).astype(BF16)

        size, start = (4, 0) if f == 0 else (2, 4)
        for dx, dz in XZ_FAR_FIRST:
            di = (x + dx) % 4 * 4 + (z + dz) % 4
            pltpu.make_async_remote_copy(
                src_ref=recv_t.at[pl.ds(base + di * size, size)], dst_ref=final.at[pl.ds(start, size), i],
                send_sem=send_c, recv_sem=recv_c, device_id=(di, j), device_id_type=MESH,
            ).start()
        src = recv_t.at[pl.ds(base + i * size, size)]
        pltpu.make_async_copy(src, final.at[pl.ds(start, size), i], recv_c).start()

    for _ in range(4):
        pltpu.make_async_copy(tokens.at[0], xin.at[0, 0], send_a.at[1]).wait()
    for _ in range(6):
        pltpu.make_async_copy(tokens.at[0], xin.at[0, 0], send_f).wait()
    pltpu.make_async_copy(mix_out_0, mix_out_0, send_m.at[0]).wait()
    for _ in range(3):
        pltpu.make_async_copy(mix_out_1.at[0], mix_out_1.at[0], send_m.at[1]).wait()

    @pl.loop(0, 64 - core)
    def _(n):
        pltpu.make_async_copy(recv_t.at[0], recv_t.at[0], send_b.at[0]).wait()

    self_sent = jnp.where(jnp.logical_and(core == 1, pair == member), 1, 0)

    @pl.loop(0, 32 - self_sent)
    def _(n):
        pltpu.make_async_copy(recv_t.at[0], recv_t.at[0], send_b.at[1]).wait()

    @pl.loop(0, 15)
    def _(n):
        pltpu.make_async_copy(recv_t.at[pl.ds(0, 6)], recv_t.at[pl.ds(0, 6)], send_c).wait()

    pltpu.make_async_copy(final, final, recv_c).wait()


def body(tokens, clip_ids, modulation, w_spatial_qkv, w_spatial_out, w_temporal_qkv, w_temporal_out):
    any_, vmem = pl.BlockSpec(memory_space=pl.ANY), pl.BlockSpec(memory_space=pltpu.VMEM)
    dma = pltpu.SemaphoreType.DMA
    final = pl.pallas_call(
        kernel,
        out_shape=jax.ShapeDtypeStruct((6, 16, 8, D), BF16),
        in_specs=[any_, vmem, vmem, any_, any_, any_, any_],
        out_specs=any_,
        scratch_shapes=[
            pltpu.VMEM((2, 8, 128, D), BF16),
            pltpu.VMEM((D, 3 * D), BF16),
            pltpu.VMEM((D, 1920), BF16),
            pltpu.VMEM((D, D), BF16),
            pltpu.VMEM((D, D), BF16),
            pltpu.VMEM((640, 128), F32),
            pltpu.VMEM((640, 256), F32),
            pltpu.VMEM((HEADS // 2, WIN, 1024), BF16),
            pltpu.VMEM((1024, 640), BF16),
            pltpu.VMEM((HEADS // 2, HD + 8, 1024), BF16),
            pltpu.VMEM((2, 1024, 512), F32),
            pltpu.VMEM((2, 1024, 512), BF16),
            pltpu.VMEM((D // 2, 512), F32),
            pltpu.VMEM((D // 2, 512), BF16),
            pltpu.VMEM((3, D // 4, 256), BF16),
            pltpu.VMEM((D, 512), BF16),
            pltpu.VMEM((D, 256), BF16),
            pltpu.VMEM((2, 8, 8, 8, D), BF16),
            pltpu.VMEM((96, 8, D), BF16),
            pltpu.VMEM((9, 768, 128), F32),
            pltpu.VMEM((512, D), BF16),
            pltpu.VMEM((256, D), BF16),
            pltpu.VMEM((512, 3 * D), BF16),
            pltpu.VMEM((256, 3 * D), BF16),
            pltpu.VMEM((3, 96, D), F32),
            dma((2,)), dma((2, 8)), dma, dma((2,)), dma((2,)), dma((2,)), dma((2,)), dma, dma, dma((9,)),
            pltpu.SemaphoreType.REGULAR,
        ],
        compiler_params=pltpu.CompilerParams(
            collective_id=0, has_side_effects=True, vmem_limit_bytes=63 * 1024 * 1024
        ),
        name="block",
    )(
        tokens, clip_ids.reshape(1, 96), modulation.transpose(1, 0, 2),
        w_spatial_qkv, w_spatial_out, w_temporal_qkv, w_temporal_out,
    )
    return final.reshape(6, 128, D)


def solution(mesh):
    in_specs = (P("frame", "inframe", None), P(), P(), P(), P(), P(), P())
    out_specs = P("frame", "inframe", None)
    return jax.shard_map(body, mesh=mesh, in_specs=in_specs, out_specs=out_specs, check_vma=False)
```

```python
import math

import jax
import jax.numpy as jnp
from jax import lax
from jax.experimental import pallas as pl
from jax.experimental.pallas import tpu as pltpu
from jax.sharding import PartitionSpec as P

MESH = pl.DeviceIdType.MESH
F32, BF16 = jnp.float32, jnp.bfloat16
HEADS = 16
HD = 72
D = HEADS * HD
WIN = 256
Q_SCALE = HD**-0.5 / math.log(2.0)
NEG = -1e30


YZ_FAR_FIRST = [(2, 2), (1, 2), (2, 1), (3, 2), (2, 3), (1, 1), (3, 3), (1, 3), (3, 1), (2, 0), (0, 2)]
YZ_FAR_FIRST += [(1, 0), (0, 1), (3, 0), (0, 3), (0, 0)]
XZ_FAR_FIRST = YZ_FAR_FIRST[:-1]


def normed(x, shift, scale):
    center = x - jnp.mean(x, axis=-1, keepdims=True)
    spread = jnp.mean(center * center, axis=-1, keepdims=True)
    return (center * lax.rsqrt(spread + 1e-06) * (1.0 + scale) + shift).astype(BF16)


def dot(a, b):
    return jnp.dot(a, b, preferred_element_type=F32)


def dot_t(a, b):
    return lax.dot_general(a, b, (((1,), (1,)), ((), ())), preferred_element_type=F32)


def window(h):
    return min(h * HD // 128, 7) * 128


def kernel(
    tokens, clips, mod, wsq, wso, wtq, wto,
    final,
    xin, wq, ws, wo, wo2, qtf, vtf, qt_s, k_s, vt_s, score, power, mixt, mix_out_0, mix_out_1, mix_0, mix_1,
    first_out, recv_t, f32_t,
    rows_a, rows_b, qkv_a, qkv_b, mods_t,
    send_a, recv_a, send_f, send_m, recv_m, send_b, recv_b, send_c, recv_c, w_sem, all_in,
):
    i = lax.axis_index("frame")
    j = lax.axis_index("inframe")
    x, z = i // 4, i % 4
    y, core = j // 2, j % 2
    sibling = y * 2 + 1 - core

    pair, member = y // 2, y % 2

    def weight_copy(src, dst, n):
        return pltpu.make_async_copy(src, dst, w_sem.at[n])

    barrier = pltpu.get_barrier_semaphore()

    @pl.loop(1, 8)
    def _(k):
        pl.semaphore_signal(barrier, inc=1, device_id=(i, (j + k) % 8), device_id_type=MESH)

    @pl.loop(1, 16)
    def _(k):
        pl.semaphore_signal(barrier, inc=1, device_id=((i + k) % 16, j), device_id_type=MESH)

    def head_columns(f):
        wide, lane_gap = (640, 512) if f == 0 else (384, 256)
        share = core if f == 0 else member * 2 + core
        return [
            weight_copy(
                wsq.at[:, pl.ds(pl.multiple_of(n * D + share * lane_gap, 128), wide)],
                ws.at[:, n * wide : n * wide + wide], 3 * f + n,
            )
            for n in range(3)
        ]

    for copy in head_columns(0):
        copy.start()
    weight_copy(wso, wo, 6).start()
    weight_copy(wto, wo2, 7).start()
    weight_copy(wtq, wq, 8).start()
    pl.semaphore_wait(barrier, 22)

    def token_copy(src, f, block, dest):
        return pltpu.make_async_remote_copy(
            src_ref=src, dst_ref=xin.at[f, block], send_sem=send_a.at[f], recv_sem=recv_a.at[f, block],
            device_id=(i, dest), device_id_type=MESH,
        )

    def send_tokens(f):
        def owned(chip):
            return chip if f == 0 else 4 + chip // 2

        for dy in (2, 1, 3):
            chip = (y + dy) % 4
            token_copy(tokens.at[owned(chip)], f, j, chip * 2 + core).start()
        token_copy(tokens.at[owned(y)], f, j, sibling).start()
        pltpu.make_async_copy(tokens.at[owned(y)], xin.at[f, j], recv_a.at[f, j]).start()

    send_tokens(0)

    @pl.loop(1, 8)
    def _(k):
        pl.semaphore_signal(all_in, inc=1, device_id=(i, (j + k) % 8), device_id_type=MESH)

    def frame_at(slot):
        late = slot - 64
        return jnp.where(slot < 64, slot // 4 * 6 + slot % 4, late // 2 * 6 + 4 + late % 2)

    clip_row = clips[...]
    row_id = lax.broadcasted_iota(jnp.int32, (96, 96), 0)
    col_id = lax.broadcasted_iota(jnp.int32, (96, 96), 1)
    clip_rows = jnp.broadcast_to(clip_row, (96, 96))
    clip_natural = jnp.sum(jnp.where(row_id == col_id, clip_rows, 0), axis=1, keepdims=True)
    clip_col = jnp.sum(jnp.where(frame_at(row_id) == col_id, clip_rows, 0), axis=1, keepdims=True)
    clip_slots = jnp.sum(jnp.where(row_id == frame_at(col_id), clip_natural, 0), axis=0, keepdims=True)

    @pl.loop(0, 3)
    def _(n):
        picked = jnp.zeros((96, D), F32)
        for c in range(4):
            picked = jnp.where(clip_col == c, mod[3 + n, c : c + 1, :], picked)
        mods_t[n] = picked

    vt_s[:, HD:, :] = jnp.ones((HEADS // 2, 8, 1024), BF16)

    for copy in head_columns(0):
        copy.wait()
    weight_copy(wso, wo, 6).wait()
    weight_copy(wto, wo2, 7).wait()
    weight_copy(wtq, wq, 8).wait()

    def arrived(f, block):
        pltpu.make_async_copy(tokens.at[0], xin.at[f, block], recv_a.at[f, block]).wait()

    def forward(f):
        for dy in (2, 1, 3):
            block = (y + dy) % 4 * 2 + core
            arrived(f, block)
            pltpu.make_async_remote_copy(
                src_ref=xin.at[f, block], dst_ref=xin.at[f, block], send_sem=send_f,
                recv_sem=recv_a.at[f, block], device_id=(i, sibling), device_id_type=MESH,
            ).start()

    def send_first(f, targets):
        slot = i * 4 + y if f == 0 else 64 + i * 2 + pair
        for place_y, dz in targets:
            chip = (y + place_y) % 4 if f == 0 else member * 2 + place_y
            for k in range(2):
                for dc in range(2):
                    to_x, to_z = (x + 1 + core + 2 * k) % 4, (z + dz) % 4
                    dj = chip * 2 + (core + dc) % 2
                    src = first_out.at[f, dj, to_x // 2 * 4 + to_z]
                    copy = pltpu.make_async_remote_copy(
                        src_ref=src, dst_ref=recv_t.at[slot], send_sem=send_b.at[f],
                        recv_sem=recv_b.at[f], device_id=(to_x * 4 + to_z, dj), device_id_type=MESH,
                    )
                    if dz or dc or k == 0 or (f == 0 and place_y):
                        copy.start()
                    else:
                        here = jnp.logical_and(core == 1, chip == y)
                        pl.when(jnp.logical_not(here))(copy.start)
                        pl.when(here)(pltpu.make_async_copy(src, recv_t.at[slot], recv_b.at[f]).start)

    def spatial(f):
        heads, wide = (8, 640) if f == 0 else (4, 384)
        share = core if f == 0 else member * 2 + core
        features = heads * HD
        lane_gap = 512 if f == 0 else 256
        frame = i * 6 + (y if f == 0 else 4 + pair)
        own_clip = jnp.sum(jnp.where(lane96 == frame, clip_row, 0), axis=1, keepdims=True)

        def own_mod(n):
            picked = jnp.zeros((1, D), F32)
            for c in range(4):
                picked = jnp.where(own_clip == c, mod[n, c : c + 1, :], picked)
            return picked

        shift, scale, gate = own_mod(0), own_mod(1), own_mod(2)

        def place(h):
            low = share * (features - lane_gap) + h * HD
            return low, pl.multiple_of(jnp.minimum(low // 128, wide // 128 - 2) * 128, 128)

        arrived(f, j)
        if f == 1:
            for copy in head_columns(1):
                copy.wait()

        @pl.loop(0, 4)
        def _(s):
            yy = (y + jnp.where(s == 0, 0, jnp.where(s == 1, 2, jnp.where(s == 2, 1, 3)))) % 4

            if f == 0:
                @pl.when(s == 1)
                def _():
                    for _ in range(4):
                        pltpu.make_async_copy(tokens.at[0], xin.at[0, 0], send_a.at[0]).wait()
                    send_tokens(1)
                    forward(0)

            arrived(f, yy * 2 + 1 - core)
            rows = xin[f, pl.ds(2 * yy, 2)].astype(F32).reshape(256, D)
            hidden = normed(rows, shift, scale)
            at = pl.ds(pl.multiple_of(yy * 256, 256), 256)

            qkv = dot(hidden, ws[:, : 3 * wide])
            q = (qkv[:, :wide] * Q_SCALE).reshape(2, 2, 2, 32, wide)
            for par in range(2):
                qtf[:wide] = q[:, :, par].reshape(128, wide).T
                start = par * 512 + yy * 128 if f == 0 else yy // 2 * 512 + par * 256 + yy % 2 * 128
                cols = pl.ds(pl.multiple_of(start, 128), 128)
                for h in range(heads):
                    low, off = place(h)
                    row = lax.broadcasted_iota(jnp.int32, (WIN, 1), 0) + (off - low)
                    inside = jnp.logical_and(row >= 0, row < HD)
                    qt_s[h, :, cols] = jnp.where(inside, qtf[pl.ds(off, WIN), :], 0.0).astype(BF16)
            k_s[at, :wide] = qkv[:, wide : 2 * wide].astype(BF16)
            vtf[:wide] = qkv[:, 2 * wide :].T
            for h in range(heads):
                low, _ = place(h)
                vt_s[h, :HD, at] = vtf[pl.ds(pl.multiple_of(low, 8), HD), :].astype(BF16)

        if f == 0:
            for copy in head_columns(1):
                copy.start()

        own_rows = pl.ds(pl.multiple_of(share * features, features), features)
        mix_f = mix_0 if f == 0 else mix_1

        def hand_over(src, dest):
            pltpu.make_async_remote_copy(
                src_ref=src, dst_ref=mix_f.at[own_rows], send_sem=send_m.at[f], recv_sem=recv_m.at[f],
                device_id=(i, dest), device_id_type=MESH,
            ).start()

        @pl.loop(0, 2)
        def _(n):
            block = (x + n - core + 2) % 2 if f == 0 else (member + 1 + n) % 2
            cols = pl.ds(pl.multiple_of(block * 512, 512), 512)

            def scores(h, buf):
                _, off = place(h)
                score[buf] = dot(k_s[:, pl.ds(off, WIN)], qt_s[h, :, cols])

            def attend(h, buf):
                values = score[buf]
                top = jnp.max(values, axis=0, keepdims=True)
                power[buf] = jnp.exp2(values - top).astype(BF16)
                out = dot(vt_s[h], power[buf])
                mixt[pl.ds(pl.multiple_of(h * HD, 8), HD), :] = out[:HD] * (1.0 / out[HD : HD + 1])

            scores(0, 0)

            @pl.loop(0, heads // 2)
            def _(u):
                scores(2 * u + 1, 1)
                attend(2 * u, 0)
                scores(jnp.minimum(2 * u + 2, heads - 1), 0)
                attend(2 * u + 1, 1)

            if f == 0:
                @pl.when(n == 0)
                def _():
                    mix_out_0[...] = mixt[...].astype(BF16)
                    hand_over(mix_out_0, sibling)

                @pl.when(n == 1)
                def _():
                    mix_0[own_rows, :] = mixt[...].astype(BF16)
            else:
                there = y + 1 - 2 * member
                for par in range(2):
                    part = mixt[:features, par * 256 : par * 256 + 256].astype(BF16)
                    to_core = (par + x + 1) % 2

                    @pl.when(n == 0)
                    def _(par=par, part=part, to_core=to_core):
                        mix_out_1[par] = part
                        hand_over(mix_out_1.at[par], there * 2 + to_core)

                    @pl.when(jnp.logical_and(n == 1, to_core == core))
                    def _(part=part):
                        mix_1[own_rows, :] = part

                    @pl.when(jnp.logical_and(n == 1, to_core != core))
                    def _(part=part):
                        mix_out_1[2] = part
                        hand_over(mix_out_1.at[2], sibling)

        if f == 0:
            forward(1)
        arriving = mix_out_0 if f == 0 else mix_out_1
        pltpu.make_async_copy(arriving, arriving, recv_m.at[f]).wait()
        par = (x + core + 1) % 2

        def finish(b, mixed):
            proj = dot(mixed.astype(F32).T.astype(BF16), wo[...]).reshape(4, 2, 32, D)
            devs = pl.ds(4 * b, 4)
            for a in range(2):
                at = pl.ds(pl.multiple_of(a * 64 + par * 32, 32), 32)
                first = xin[f, devs, at, :].astype(F32) + gate * proj[:, a]
                first_out[f, devs, a * 4 : a * 4 + 4] = first.reshape(4, 4, 8, D).astype(BF16)

        if f == 0:
            @pl.loop(0, 2)
            def _(b):
                finish(b, mix_0[:, pl.ds(pl.multiple_of(b * 256, 256), 256)])

            pl.semaphore_wait(all_in, 7)
            send_first(0, YZ_FAR_FIRST)
        else:
            finish(member, mix_1[...])
            send_first(1, [(e, dz) for dz in (2, 1, 3, 0) for e in range(2)])

    lane96 = lax.broadcasted_iota(jnp.int32, (1, 96), 1)
    spatial(0)
    spatial(1)

    parts = ((0, 64, rows_a, qkv_a), (64, 32, rows_b, qkv_b))

    for f, (base, n, rows_f, qkv_f) in enumerate(parts):
        slots = recv_t.at[pl.ds(base, n)]
        pltpu.make_async_copy(slots, slots, recv_b.at[f]).wait()

        @pl.loop(0, n // 8)
        def _(c, base=base):
            rows = recv_t[pl.ds(base + c * 8, 8)].astype(F32).reshape(64, D)
            for b in range(9):
                f32_t[b, pl.ds(pl.multiple_of(base * 8 + c * 64, 64), 64), :] = rows[:, b * 128 : b * 128 + 128]

        @pl.loop(0, 8)
        def _(p, base=base, n=n, rows_f=rows_f):
            rows = jnp.concatenate([f32_t[b, pl.ds(base * 8 + p, n, stride=8), :] for b in range(9)], axis=1)
            at = pl.ds(pl.multiple_of(p * n, n), n)
            rows_f[at, :] = normed(rows, mods_t[0, base : base + n, :], mods_t[1, base : base + n, :])

        hidden = rows_f[...]
        qkv_f[:, :D] = (dot(hidden, wq[:, :D]) * Q_SCALE).astype(BF16)
        qkv_f[:, D:] = dot(hidden, wq[:, D:]).astype(BF16)

    same = clip_col == clip_slots

    def attend_position(p):
        at_a = pl.ds(pl.multiple_of(p * 64, 64), 64)
        at_b = pl.ds(pl.multiple_of(p * 32, 32), 32)
        blocks = [jnp.zeros((96, 128), F32) for _ in range(9)]
        for h in range(HEADS):
            off = window(h)
            lane = lax.broadcasted_iota(jnp.int32, (1, WIN), 1) + (off - h * HD)
            inside = jnp.logical_and(lane >= 0, lane < HD)

            def part(m):
                cols = slice(m * D + off, m * D + off + WIN)
                return jnp.concatenate([qkv_a[at_a, cols], qkv_b[at_b, cols]], axis=0)

            q = part(0)
            q = jnp.where(inside, q, jnp.zeros_like(q))
            scores = jnp.where(same, dot_t(q, part(1)), NEG)
            powers = jnp.exp2(scores - jnp.max(scores, axis=-1, keepdims=True))
            total = jnp.sum(powers, axis=-1, keepdims=True)
            out = dot(powers.astype(BF16), part(2)) * (1.0 / total)
            for b in range(off // 128, off // 128 + 2):
                lanes = slice(b * 128 - off, b * 128 - off + 128)
                blocks[b] = jnp.where(inside[:, lanes], out[:, lanes], blocks[b])
        for b in range(9):
            cols = slice(b * 128, b * 128 + 128)
            rows_a[at_a, cols] = blocks[b][:64].astype(BF16)
            rows_b[at_b, cols] = blocks[b][64:].astype(BF16)

    @pl.loop(0, 4)
    def _(u):
        attend_position(2 * u)
        attend_position(2 * u + 1)

    for f, (base, n, rows_f, _) in enumerate(parts):
        proj = dot(rows_f[...], wo2[...])
        for p in range(8):
            at = pl.ds(base * 8 + p, n, stride=8)
            for b in range(9):
                cols = slice(b * 128, b * 128 + 128)
                f32_t[b, at, :] = f32_t[b, at, :] + mods_t[2, base : base + n, cols] * proj[p * n : p * n + n, cols]

        @pl.loop(0, n // 8)
        def _(c, base=base):
            at = pl.ds(pl.multiple_of(base * 8 + c * 64, 64), 64)
            rows = jnp.concatenate([f32_t[b, at, :] for b in range(9)], axis=1)
            recv_t[pl.ds(base + c * 8, 8)] = rows.reshape(8, 8, D).astype(BF16)

        size, start = (4, 0) if f == 0 else (2, 4)
        for dx, dz in XZ_FAR_FIRST:
            di = (x + dx) % 4 * 4 + (z + dz) % 4
            pltpu.make_async_remote_copy(
                src_ref=recv_t.at[pl.ds(base + di * size, size)], dst_ref=final.at[pl.ds(start, size), i],
                send_sem=send_c, recv_sem=recv_c, device_id=(di, j), device_id_type=MESH,
            ).start()
        src = recv_t.at[pl.ds(base + i * size, size)]
        pltpu.make_async_copy(src, final.at[pl.ds(start, size), i], recv_c).start()

    for _ in range(4):
        pltpu.make_async_copy(tokens.at[0], xin.at[0, 0], send_a.at[1]).wait()
    for _ in range(6):
        pltpu.make_async_copy(tokens.at[0], xin.at[0, 0], send_f).wait()
    pltpu.make_async_copy(mix_out_0, mix_out_0, send_m.at[0]).wait()
    for _ in range(3):
        pltpu.make_async_copy(mix_out_1.at[0], mix_out_1.at[0], send_m.at[1]).wait()

    @pl.loop(0, 64 - core)
    def _(n):
        pltpu.make_async_copy(recv_t.at[0], recv_t.at[0], send_b.at[0]).wait()

    self_sent = jnp.where(jnp.logical_and(core == 1, pair == member), 1, 0)

    @pl.loop(0, 32 - self_sent)
    def _(n):
        pltpu.make_async_copy(recv_t.at[0], recv_t.at[0], send_b.at[1]).wait()

    @pl.loop(0, 15)
    def _(n):
        pltpu.make_async_copy(recv_t.at[pl.ds(0, 6)], recv_t.at[pl.ds(0, 6)], send_c).wait()

    pltpu.make_async_copy(final, final, recv_c).wait()


def body(tokens, clip_ids, modulation, w_spatial_qkv, w_spatial_out, w_temporal_qkv, w_temporal_out):
    any_, vmem = pl.BlockSpec(memory_space=pl.ANY), pl.BlockSpec(memory_space=pltpu.VMEM)
    dma = pltpu.SemaphoreType.DMA
    final = pl.pallas_call(
        kernel,
        out_shape=jax.ShapeDtypeStruct((6, 16, 8, D), BF16),
        in_specs=[any_, vmem, vmem, any_, any_, any_, any_],
        out_specs=any_,
        scratch_shapes=[
            pltpu.VMEM((2, 8, 128, D), BF16),
            pltpu.VMEM((D, 3 * D), BF16),
            pltpu.VMEM((D, 1920), BF16),
            pltpu.VMEM((D, D), BF16),
            pltpu.VMEM((D, D), BF16),
            pltpu.VMEM((640, 128), F32),
            pltpu.VMEM((640, 256), F32),
            pltpu.VMEM((HEADS // 2, WIN, 1024), BF16),
            pltpu.VMEM((1024, 640), BF16),
            pltpu.VMEM((HEADS // 2, HD + 8, 1024), BF16),
            pltpu.VMEM((2, 1024, 512), F32),
            pltpu.VMEM((2, 1024, 512), BF16),
            pltpu.VMEM((D // 2, 512), F32),
            pltpu.VMEM((D // 2, 512), BF16),
            pltpu.VMEM((3, D // 4, 256), BF16),
            pltpu.VMEM((D, 512), BF16),
            pltpu.VMEM((D, 256), BF16),
            pltpu.VMEM((2, 8, 8, 8, D), BF16),
            pltpu.VMEM((96, 8, D), BF16),
            pltpu.VMEM((9, 768, 128), F32),
            pltpu.VMEM((512, D), BF16),
            pltpu.VMEM((256, D), BF16),
            pltpu.VMEM((512, 3 * D), BF16),
            pltpu.VMEM((256, 3 * D), BF16),
            pltpu.VMEM((3, 96, D), F32),
            dma((2,)), dma((2, 8)), dma, dma((2,)), dma((2,)), dma((2,)), dma((2,)), dma, dma, dma((9,)),
            pltpu.SemaphoreType.REGULAR,
        ],
        compiler_params=pltpu.CompilerParams(
            collective_id=0, has_side_effects=True, vmem_limit_bytes=63 * 1024 * 1024
        ),
        name="block",
    )(
        tokens, clip_ids.reshape(1, 96), modulation.transpose(1, 0, 2),
        w_spatial_qkv, w_spatial_out, w_temporal_qkv, w_temporal_out,
    )
    return final.reshape(6, 128, D)


def solution(mesh):
    in_specs = (P("frame", "inframe", None), P(), P(), P(), P(), P(), P())
    out_specs = P("frame", "inframe", None)
    return jax.shard_map(body, mesh=mesh, in_specs=in_specs, out_specs=out_specs, check_vma=False)
```

```python
import math

import jax
import jax.numpy as jnp
from jax import lax
from jax.experimental import pallas as pl
from jax.experimental.pallas import tpu as pltpu
from jax.sharding import PartitionSpec as P

MESH = pl.DeviceIdType.MESH
F32, BF16 = jnp.float32, jnp.bfloat16
HEADS = 16
HD = 72
D = HEADS * HD
WIN = 256
Q_SCALE = HD**-0.5 / math.log(2.0)
NEG = -1e30


YZ_FAR_FIRST = [(2, 2), (1, 2), (2, 1), (3, 2), (2, 3), (1, 1), (3, 3), (1, 3), (3, 1), (2, 0), (0, 2)]
YZ_FAR_FIRST += [(1, 0), (0, 1), (3, 0), (0, 3), (0, 0)]
XZ_FAR_FIRST = YZ_FAR_FIRST[:-1]


def normed(x, shift, scale):
    center = x - jnp.mean(x, axis=-1, keepdims=True)
    spread = jnp.mean(center * center, axis=-1, keepdims=True)
    return (center * lax.rsqrt(spread + 1e-06) * (1.0 + scale) + shift).astype(BF16)


def dot(a, b):
    return jnp.dot(a, b, preferred_element_type=F32)


def dot_t(a, b):
    return lax.dot_general(a, b, (((1,), (1,)), ((), ())), preferred_element_type=F32)


def window(h):
    return min(h * HD // 128, 7) * 128


def kernel(
    tokens, clips, mod, wsq, wso, wtq, wto,
    final,
    xin, wq, ws, wo, wo2, qtf, vtf, qt_s, k_s, vt_s, score, power, mixt, mix_out_0, mix_out_1, mix_0, mix_1,
    first_out, recv_t, f32_t,
    rows_a, rows_b, qkv_a, qkv_b, mods_t,
    send_a, recv_a, send_f, send_m, recv_m, send_b, recv_b, send_c, recv_c, w_sem, all_in,
):
    i = lax.axis_index("frame")
    j = lax.axis_index("inframe")
    x, z = i // 4, i % 4
    y, core = j // 2, j % 2
    sibling = y * 2 + 1 - core

    pair, member = y // 2, y % 2

    def weight_copy(src, dst, n):
        return pltpu.make_async_copy(src, dst, w_sem.at[n])

    barrier = pltpu.get_barrier_semaphore()

    @pl.loop(1, 8)
    def _(k):
        pl.semaphore_signal(barrier, inc=1, device_id=(i, (j + k) % 8), device_id_type=MESH)

    @pl.loop(1, 16)
    def _(k):
        pl.semaphore_signal(barrier, inc=1, device_id=((i + k) % 16, j), device_id_type=MESH)

    def head_columns(f):
        wide, lane_gap = (640, 512) if f == 0 else (384, 256)
        share = core if f == 0 else member * 2 + core
        return [
            weight_copy(
                wsq.at[:, pl.ds(pl.multiple_of(n * D + share * lane_gap, 128), wide)],
                ws.at[:, n * wide : n * wide + wide], 3 * f + n,
            )
            for n in range(3)
        ]

    for copy in head_columns(0):
        copy.start()
    weight_copy(wso, wo, 6).start()
    weight_copy(wto, wo2, 7).start()
    weight_copy(wtq, wq, 8).start()
    pl.semaphore_wait(barrier, 22)

    def token_copy(src, f, block, dest):
        return pltpu.make_async_remote_copy(
            src_ref=src, dst_ref=xin.at[f, block], send_sem=send_a.at[f], recv_sem=recv_a.at[f, block],
            device_id=(i, dest), device_id_type=MESH,
        )

    def send_tokens(f):
        def owned(chip):
            return chip if f == 0 else 4 + chip // 2

        for dy in (2, 1, 3):
            chip = (y + dy) % 4
            token_copy(tokens.at[owned(chip)], f, j, chip * 2 + core).start()
        token_copy(tokens.at[owned(y)], f, j, sibling).start()
        pltpu.make_async_copy(tokens.at[owned(y)], xin.at[f, j], recv_a.at[f, j]).start()

    send_tokens(0)

    @pl.loop(1, 8)
    def _(k):
        pl.semaphore_signal(all_in, inc=1, device_id=(i, (j + k) % 8), device_id_type=MESH)

    def frame_at(slot):
        late = slot - 64
        return jnp.where(slot < 64, slot // 4 * 6 + slot % 4, late // 2 * 6 + 4 + late % 2)

    clip_row = clips[...]
    row_id = lax.broadcasted_iota(jnp.int32, (96, 96), 0)
    col_id = lax.broadcasted_iota(jnp.int32, (96, 96), 1)
    clip_rows = jnp.broadcast_to(clip_row, (96, 96))
    clip_natural = jnp.sum(jnp.where(row_id == col_id, clip_rows, 0), axis=1, keepdims=True)
    clip_col = jnp.sum(jnp.where(frame_at(row_id) == col_id, clip_rows, 0), axis=1, keepdims=True)
    clip_slots = jnp.sum(jnp.where(row_id == frame_at(col_id), clip_natural, 0), axis=0, keepdims=True)

    @pl.loop(0, 3)
    def _(n):
        picked = jnp.zeros((96, D), F32)
        for c in range(4):
            picked = jnp.where(clip_col == c, mod[3 + n, c : c + 1, :], picked)
        mods_t[n] = picked

    vt_s[:, HD:, :] = jnp.ones((HEADS // 2, 8, 1024), BF16)

    for copy in head_columns(0):
        copy.wait()
    weight_copy(wso, wo, 6).wait()
    weight_copy(wto, wo2, 7).wait()
    weight_copy(wtq, wq, 8).wait()

    def arrived(f, block):
        pltpu.make_async_copy(tokens.at[0], xin.at[f, block], recv_a.at[f, block]).wait()

    def forward(f):
        for dy in (2, 1, 3):
            block = (y + dy) % 4 * 2 + core
            arrived(f, block)
            pltpu.make_async_remote_copy(
                src_ref=xin.at[f, block], dst_ref=xin.at[f, block], send_sem=send_f,
                recv_sem=recv_a.at[f, block], device_id=(i, sibling), device_id_type=MESH,
            ).start()

    def send_first(f, targets):
        slot = i * 4 + y if f == 0 else 64 + i * 2 + pair
        for place_y, dz in targets:
            chip = (y + place_y) % 4 if f == 0 else member * 2 + place_y
            for k in range(2):
                for dc in range(2):
                    to_x, to_z = (x + 1 + core + 2 * k) % 4, (z + dz) % 4
                    dj = chip * 2 + (core + dc) % 2
                    src = first_out.at[f, dj, to_x // 2 * 4 + to_z]
                    copy = pltpu.make_async_remote_copy(
                        src_ref=src, dst_ref=recv_t.at[slot], send_sem=send_b.at[f],
                        recv_sem=recv_b.at[f], device_id=(to_x * 4 + to_z, dj), device_id_type=MESH,
                    )
                    if dz or dc or k == 0 or (f == 0 and place_y):
                        copy.start()
                    else:
                        here = jnp.logical_and(core == 1, chip == y)
                        pl.when(jnp.logical_not(here))(copy.start)
                        pl.when(here)(pltpu.make_async_copy(src, recv_t.at[slot], recv_b.at[f]).start)

    def spatial(f):
        heads, wide = (8, 640) if f == 0 else (4, 384)
        share = core if f == 0 else member * 2 + core
        features = heads * HD
        lane_gap = 512 if f == 0 else 256
        frame = i * 6 + (y if f == 0 else 4 + pair)
        own_clip = jnp.sum(jnp.where(lane96 == frame, clip_row, 0), axis=1, keepdims=True)

        def own_mod(n):
            picked = jnp.zeros((1, D), F32)
            for c in range(4):
                picked = jnp.where(own_clip == c, mod[n, c : c + 1, :], picked)
            return picked

        shift, scale, gate = own_mod(0), own_mod(1), own_mod(2)

        def place(h):
            low = share * (features - lane_gap) + h * HD
            return low, pl.multiple_of(jnp.minimum(low // 128, wide // 128 - 2) * 128, 128)

        arrived(f, j)
        if f == 1:
            for copy in head_columns(1):
                copy.wait()

        def project_chip(s, e):
            yy = (y + jnp.where(s == 0, 0, jnp.where(s == 1, 2, jnp.where(s == 2, 1, 3)))) % 4

            if f == 0:
                @pl.when(s == 1)
                def _():
                    for _ in range(4):
                        pltpu.make_async_copy(tokens.at[0], xin.at[0, 0], send_a.at[0]).wait()
                    send_tokens(1)
                    forward(0)

            arrived(f, yy * 2 + 1 - core)
            rows = xin[f, pl.ds(2 * yy, 2)].astype(F32).reshape(256, D)
            hidden = normed(rows, shift, scale)
            at = pl.ds(pl.multiple_of(yy * 256, 256), 256)

            qkv = dot(hidden, ws[:, : 3 * wide])
            q = (qkv[:, :wide] * Q_SCALE).reshape(2, 2, 2, 32, wide)
            for par in range(2):
                qtf[2 * e + par, :wide] = q[:, :, par].reshape(128, wide).T
                start = par * 512 + yy * 128 if f == 0 else yy // 2 * 512 + par * 256 + yy % 2 * 128
                cols = pl.ds(pl.multiple_of(start, 128), 128)
                for h in range(heads):
                    low, off = place(h)
                    row = lax.broadcasted_iota(jnp.int32, (WIN, 1), 0) + (off - low)
                    inside = jnp.logical_and(row >= 0, row < HD)
                    qt_s[h, :, cols] = jnp.where(inside, qtf[2 * e + par, pl.ds(off, WIN), :], 0.0).astype(BF16)
            k_s[at, :wide] = qkv[:, wide : 2 * wide].astype(BF16)
            vtf[e, :wide] = qkv[:, 2 * wide :].T
            for h in range(heads):
                low, _ = place(h)
                vt_s[h, :HD, at] = vtf[e, pl.ds(pl.multiple_of(low, 8), HD), :].astype(BF16)

        @pl.loop(0, 4 if f == 0 else 2)
        def _(u):
            if f == 0:
                project_chip(u, 0)
            else:
                project_chip(2 * u, 0)
                project_chip(2 * u + 1, 1)

        if f == 0:
            for copy in head_columns(1):
                copy.start()

        own_rows = pl.ds(pl.multiple_of(share * features, features), features)
        mix_f = mix_0 if f == 0 else mix_1

        def hand_over(src, dest, rows=own_rows):
            pltpu.make_async_remote_copy(
                src_ref=src, dst_ref=mix_f.at[rows], send_sem=send_m.at[f], recv_sem=recv_m.at[f],
                device_id=(i, dest), device_id_type=MESH,
            ).start()

        @pl.loop(0, 2)
        def _(n):
            block = (x + n - core + 2) % 2 if f == 0 else (member + 1 + n) % 2
            cols = pl.ds(pl.multiple_of(block * 512, 512), 512)

            def scores(h, buf):
                _, off = place(h)
                score[buf] = dot(k_s[:, pl.ds(off, WIN)], qt_s[h, :, cols])

            def attend(h, buf):
                values = score[buf]
                top = jnp.max(values, axis=0, keepdims=True)
                power[buf] = jnp.exp2(values - top).astype(BF16)
                out = dot(vt_s[h], power[buf])
                mixt[pl.ds(pl.multiple_of(h * HD, 8), HD), :] = out[:HD] * (1.0 / out[HD : HD + 1])

            scores(0, 0)

            @pl.loop(0, heads // 2)
            def _(u):
                scores(2 * u + 1, 1)
                attend(2 * u, 0)
                scores(jnp.minimum(2 * u + 2, heads - 1), 0)
                attend(2 * u + 1, 1)

                if f == 1:
                    @pl.when(n == 0)
                    def _():
                        done = pl.ds(pl.multiple_of(u * 2 * HD, 2 * HD), 2 * HD)
                        rows = pl.ds(pl.multiple_of(share * features + u * 2 * HD, 2 * HD), 2 * HD)
                        for par in range(2):
                            mix_out_1[par, done, :] = mixt[done, par * 256 : par * 256 + 256].astype(BF16)
                            to_core = (par + x + 1) % 2
                            hand_over(mix_out_1.at[par, done], (y + 1 - 2 * member) * 2 + to_core, rows)

            if f == 0:
                @pl.when(n == 0)
                def _():
                    mix_out_0[...] = mixt[...].astype(BF16)
                    hand_over(mix_out_0, sibling)

                @pl.when(n == 1)
                def _():
                    mix_0[own_rows, :] = mixt[...].astype(BF16)
            else:
                for par in range(2):
                    part = mixt[:features, par * 256 : par * 256 + 256].astype(BF16)
                    to_core = (par + x + 1) % 2

                    @pl.when(jnp.logical_and(n == 1, to_core == core))
                    def _(part=part):
                        mix_1[own_rows, :] = part

                    @pl.when(jnp.logical_and(n == 1, to_core != core))
                    def _(part=part):
                        mix_out_1[2] = part
                        hand_over(mix_out_1.at[2], sibling)

        if f == 0:
            forward(1)
        arriving = mix_out_0 if f == 0 else mix_out_1
        pltpu.make_async_copy(arriving, arriving, recv_m.at[f]).wait()
        par = (x + core + 1) % 2

        def finish(b, mixed):
            proj = dot(mixed.astype(F32).T.astype(BF16), wo[...]).reshape(4, 2, 32, D)
            devs = pl.ds(4 * b, 4)
            for a in range(2):
                at = pl.ds(pl.multiple_of(a * 64 + par * 32, 32), 32)
                first = xin[f, devs, at, :].astype(F32) + gate * proj[:, a]
                first_out[f, devs, a * 4 : a * 4 + 4] = first.reshape(4, 4, 8, D).astype(BF16)

        if f == 0:
            @pl.loop(0, 2)
            def _(b):
                finish(b, mix_0[:, pl.ds(pl.multiple_of(b * 256, 256), 256)])

            pl.semaphore_wait(all_in, 7)
            send_first(0, YZ_FAR_FIRST)
        else:
            finish(member, mix_1[...])
            send_first(1, [(e, dz) for dz in (2, 1, 3, 0) for e in range(2)])

    lane96 = lax.broadcasted_iota(jnp.int32, (1, 96), 1)
    spatial(0)
    spatial(1)

    parts = ((0, 64, rows_a, qkv_a), (64, 32, rows_b, qkv_b))

    for f, (base, n, rows_f, qkv_f) in enumerate(parts):
        slots = recv_t.at[pl.ds(base, n)]
        pltpu.make_async_copy(slots, slots, recv_b.at[f]).wait()

        @pl.loop(0, n // 8)
        def _(c, base=base):
            rows = recv_t[pl.ds(base + c * 8, 8)].astype(F32).reshape(64, D)
            for b in range(9):
                f32_t[b, pl.ds(pl.multiple_of(base * 8 + c * 64, 64), 64), :] = rows[:, b * 128 : b * 128 + 128]

        @pl.loop(0, 8, unroll=4)
        def _(p, base=base, n=n, rows_f=rows_f):
            rows = jnp.concatenate([f32_t[b, pl.ds(base * 8 + p, n, stride=8), :] for b in range(9)], axis=1)
            at = pl.ds(pl.multiple_of(p * n, n), n)
            rows_f[at, :] = normed(rows, mods_t[0, base : base + n, :], mods_t[1, base : base + n, :])

        hidden = rows_f[...]
        qkv_f[:, :D] = (dot(hidden, wq[:, :D]) * Q_SCALE).astype(BF16)
        qkv_f[:, D:] = dot(hidden, wq[:, D:]).astype(BF16)

    same = clip_col == clip_slots

    def attend_position(p):
        at_a = pl.ds(pl.multiple_of(p * 64, 64), 64)
        at_b = pl.ds(pl.multiple_of(p * 32, 32), 32)
        blocks = [jnp.zeros((96, 128), F32) for _ in range(9)]
        for h in range(HEADS):
            off = window(h)
            lane = lax.broadcasted_iota(jnp.int32, (1, WIN), 1) + (off - h * HD)
            inside = jnp.logical_and(lane >= 0, lane < HD)

            def part(m):
                cols = slice(m * D + off, m * D + off + WIN)
                return jnp.concatenate([qkv_a[at_a, cols], qkv_b[at_b, cols]], axis=0)

            q = part(0)
            q = jnp.where(inside, q, jnp.zeros_like(q))
            scores = jnp.where(same, dot_t(q, part(1)), NEG)
            powers = jnp.exp2(scores - jnp.max(scores, axis=-1, keepdims=True))
            total = jnp.sum(powers, axis=-1, keepdims=True)
            out = dot(powers.astype(BF16), part(2)) * (1.0 / total)
            for b in range(off // 128, off // 128 + 2):
                lanes = slice(b * 128 - off, b * 128 - off + 128)
                blocks[b] = jnp.where(inside[:, lanes], out[:, lanes], blocks[b])
        for b in range(9):
            cols = slice(b * 128, b * 128 + 128)
            rows_a[at_a, cols] = blocks[b][:64].astype(BF16)
            rows_b[at_b, cols] = blocks[b][64:].astype(BF16)

    @pl.loop(0, 4)
    def _(u):
        attend_position(2 * u)
        attend_position(2 * u + 1)

    for f, (base, n, rows_f, _) in enumerate(parts):
        proj = dot(rows_f[...], wo2[...])
        for p in range(8):
            at = pl.ds(base * 8 + p, n, stride=8)
            for b in range(9):
                cols = slice(b * 128, b * 128 + 128)
                f32_t[b, at, :] = f32_t[b, at, :] + mods_t[2, base : base + n, cols] * proj[p * n : p * n + n, cols]

        @pl.loop(0, n // 8)
        def _(c, base=base):
            at = pl.ds(pl.multiple_of(base * 8 + c * 64, 64), 64)
            rows = jnp.concatenate([f32_t[b, at, :] for b in range(9)], axis=1)
            recv_t[pl.ds(base + c * 8, 8)] = rows.reshape(8, 8, D).astype(BF16)

        size, start = (4, 0) if f == 0 else (2, 4)
        for dx, dz in XZ_FAR_FIRST:
            di = (x + dx) % 4 * 4 + (z + dz) % 4
            pltpu.make_async_remote_copy(
                src_ref=recv_t.at[pl.ds(base + di * size, size)], dst_ref=final.at[pl.ds(start, size), i],
                send_sem=send_c, recv_sem=recv_c, device_id=(di, j), device_id_type=MESH,
            ).start()
        src = recv_t.at[pl.ds(base + i * size, size)]
        pltpu.make_async_copy(src, final.at[pl.ds(start, size), i], recv_c).start()

    for _ in range(4):
        pltpu.make_async_copy(tokens.at[0], xin.at[0, 0], send_a.at[1]).wait()
    for _ in range(6):
        pltpu.make_async_copy(tokens.at[0], xin.at[0, 0], send_f).wait()
    pltpu.make_async_copy(mix_out_0, mix_out_0, send_m.at[0]).wait()
    for _ in range(3):
        pltpu.make_async_copy(mix_out_1.at[0], mix_out_1.at[0], send_m.at[1]).wait()

    @pl.loop(0, 64 - core)
    def _(n):
        pltpu.make_async_copy(recv_t.at[0], recv_t.at[0], send_b.at[0]).wait()

    self_sent = jnp.where(jnp.logical_and(core == 1, pair == member), 1, 0)

    @pl.loop(0, 32 - self_sent)
    def _(n):
        pltpu.make_async_copy(recv_t.at[0], recv_t.at[0], send_b.at[1]).wait()

    @pl.loop(0, 15)
    def _(n):
        pltpu.make_async_copy(recv_t.at[pl.ds(0, 6)], recv_t.at[pl.ds(0, 6)], send_c).wait()

    pltpu.make_async_copy(final, final, recv_c).wait()


def body(tokens, clip_ids, modulation, w_spatial_qkv, w_spatial_out, w_temporal_qkv, w_temporal_out):
    any_, vmem = pl.BlockSpec(memory_space=pl.ANY), pl.BlockSpec(memory_space=pltpu.VMEM)
    dma = pltpu.SemaphoreType.DMA
    final = pl.pallas_call(
        kernel,
        out_shape=jax.ShapeDtypeStruct((6, 16, 8, D), BF16),
        in_specs=[any_, vmem, vmem, any_, any_, any_, any_],
        out_specs=any_,
        scratch_shapes=[
            pltpu.VMEM((2, 8, 128, D), BF16),
            pltpu.VMEM((D, 3 * D), BF16),
            pltpu.VMEM((D, 1920), BF16),
            pltpu.VMEM((D, D), BF16),
            pltpu.VMEM((D, D), BF16),
            pltpu.VMEM((4, 640, 128), F32),
            pltpu.VMEM((2, 640, 256), F32),
            pltpu.VMEM((HEADS // 2, WIN, 1024), BF16),
            pltpu.VMEM((1024, 640), BF16),
            pltpu.VMEM((HEADS // 2, HD + 8, 1024), BF16),
            pltpu.VMEM((2, 1024, 512), F32),
            pltpu.VMEM((2, 1024, 512), BF16),
            pltpu.VMEM((D // 2, 512), F32),
            pltpu.VMEM((D // 2, 512), BF16),
            pltpu.VMEM((3, D // 4, 256), BF16),
            pltpu.VMEM((D, 512), BF16),
            pltpu.VMEM((D, 256), BF16),
            pltpu.VMEM((2, 8, 8, 8, D), BF16),
            pltpu.VMEM((96, 8, D), BF16),
            pltpu.VMEM((9, 768, 128), F32),
            pltpu.VMEM((512, D), BF16),
            pltpu.VMEM((256, D), BF16),
            pltpu.VMEM((512, 3 * D), BF16),
            pltpu.VMEM((256, 3 * D), BF16),
            pltpu.VMEM((3, 96, D), F32),
            dma((2,)), dma((2, 8)), dma, dma((2,)), dma((2,)), dma((2,)), dma((2,)), dma, dma, dma((9,)),
            pltpu.SemaphoreType.REGULAR,
        ],
        compiler_params=pltpu.CompilerParams(
            collective_id=0, has_side_effects=True, vmem_limit_bytes=63 * 1024 * 1024
        ),
        name="block",
    )(
        tokens, clip_ids.reshape(1, 96), modulation.transpose(1, 0, 2),
        w_spatial_qkv, w_spatial_out, w_temporal_qkv, w_temporal_out,
    )
    return final.reshape(6, 128, D)


def solution(mesh):
    in_specs = (P("frame", "inframe", None), P(), P(), P(), P(), P(), P())
    out_specs = P("frame", "inframe", None)
    return jax.shard_map(body, mesh=mesh, in_specs=in_specs, out_specs=out_specs, check_vma=False)
```

```python
import math

import jax
import jax.numpy as jnp
from jax import lax
from jax.experimental import pallas as pl
from jax.experimental.pallas import tpu as pltpu
from jax.sharding import PartitionSpec as P

MESH = pl.DeviceIdType.MESH
F32, BF16 = jnp.float32, jnp.bfloat16
HEADS = 16
HD = 72
D = HEADS * HD
WIN = 256
Q_SCALE = HD**-0.5 / math.log(2.0)
NEG = -1e30


YZ_FAR_FIRST = [(2, 2), (1, 2), (2, 1), (3, 2), (2, 3), (1, 1), (3, 3), (1, 3), (3, 1), (2, 0), (0, 2)]
YZ_FAR_FIRST += [(1, 0), (0, 1), (3, 0), (0, 3), (0, 0)]
XZ_FAR_FIRST = YZ_FAR_FIRST[:-1]


def normed(x, shift, scale):
    center = x - jnp.mean(x, axis=-1, keepdims=True)
    spread = jnp.mean(center * center, axis=-1, keepdims=True)
    return (center * lax.rsqrt(spread + 1e-06) * (1.0 + scale) + shift).astype(BF16)


def dot(a, b):
    return jnp.dot(a, b, preferred_element_type=F32)


def dot_t(a, b):
    return lax.dot_general(a, b, (((1,), (1,)), ((), ())), preferred_element_type=F32)


def window(h):
    return min(h * HD // 128, 7) * 128


def kernel(
    tokens, clips, mod, wsq, wso, wtq, wto,
    final,
    xin, wq, ws, wo, wo2, qtf, vtf, qt_s, k_s, vt_s, score, power, mixt, mix_out_0, mix_out_1, mix_0, mix_1,
    first_out, recv_t, f32_t,
    rows_a, rows_b, qkv_a, qkv_b, mods_t,
    send_a, recv_a, send_f, send_m, recv_m, send_b, recv_b, send_c, recv_c, w_sem, all_in,
):
    i = lax.axis_index("frame")
    j = lax.axis_index("inframe")
    x, z = i // 4, i % 4
    y, core = j // 2, j % 2
    sibling = y * 2 + 1 - core

    pair, member = y // 2, y % 2

    def weight_copy(src, dst, n):
        return pltpu.make_async_copy(src, dst, w_sem.at[n])

    barrier = pltpu.get_barrier_semaphore()

    @pl.loop(1, 8)
    def _(k):
        pl.semaphore_signal(barrier, inc=1, device_id=(i, (j + k) % 8), device_id_type=MESH)

    @pl.loop(1, 16)
    def _(k):
        pl.semaphore_signal(barrier, inc=1, device_id=((i + k) % 16, j), device_id_type=MESH)

    def head_columns(f):
        wide, lane_gap = (640, 512) if f == 0 else (384, 256)
        share = core if f == 0 else member * 2 + core
        return [
            weight_copy(
                wsq.at[:, pl.ds(pl.multiple_of(n * D + share * lane_gap, 128), wide)],
                ws.at[:, n * wide : n * wide + wide], 3 * f + n,
            )
            for n in range(3)
        ]

    for copy in head_columns(0):
        copy.start()
    weight_copy(wso, wo, 6).start()
    weight_copy(wto, wo2, 7).start()
    weight_copy(wtq, wq, 8).start()
    pl.semaphore_wait(barrier, 22)

    def token_copy(src, f, block, dest):
        return pltpu.make_async_remote_copy(
            src_ref=src, dst_ref=xin.at[f, block], send_sem=send_a.at[f], recv_sem=recv_a.at[f, block],
            device_id=(i, dest), device_id_type=MESH,
        )

    def send_tokens(f):
        def owned(chip):
            return chip if f == 0 else 4 + chip // 2

        for dy in (2, 1, 3):
            chip = (y + dy) % 4
            token_copy(tokens.at[owned(chip)], f, j, chip * 2 + core).start()
        token_copy(tokens.at[owned(y)], f, j, sibling).start()
        pltpu.make_async_copy(tokens.at[owned(y)], xin.at[f, j], recv_a.at[f, j]).start()

    send_tokens(0)

    @pl.loop(1, 8)
    def _(k):
        pl.semaphore_signal(all_in, inc=1, device_id=(i, (j + k) % 8), device_id_type=MESH)

    def frame_at(slot):
        late = slot - 64
        return jnp.where(slot < 64, slot // 4 * 6 + slot % 4, late // 2 * 6 + 4 + late % 2)

    clip_row = clips[...]
    row_id = lax.broadcasted_iota(jnp.int32, (96, 96), 0)
    col_id = lax.broadcasted_iota(jnp.int32, (96, 96), 1)
    clip_rows = jnp.broadcast_to(clip_row, (96, 96))
    clip_natural = jnp.sum(jnp.where(row_id == col_id, clip_rows, 0), axis=1, keepdims=True)
    clip_col = jnp.sum(jnp.where(frame_at(row_id) == col_id, clip_rows, 0), axis=1, keepdims=True)
    clip_slots = jnp.sum(jnp.where(row_id == frame_at(col_id), clip_natural, 0), axis=0, keepdims=True)

    @pl.loop(0, 3)
    def _(n):
        picked = jnp.zeros((96, D), F32)
        for c in range(4):
            picked = jnp.where(clip_col == c, mod[3 + n, c : c + 1, :], picked)
        mods_t[n] = picked

    vt_s[:, HD:, :] = jnp.ones((HEADS // 2, 8, 1024), BF16)

    for copy in head_columns(0):
        copy.wait()
    weight_copy(wso, wo, 6).wait()
    weight_copy(wto, wo2, 7).wait()
    weight_copy(wtq, wq, 8).wait()

    def arrived(f, block):
        pltpu.make_async_copy(tokens.at[0], xin.at[f, block], recv_a.at[f, block]).wait()

    def forward(f):
        for dy in (2, 1, 3):
            block = (y + dy) % 4 * 2 + core
            arrived(f, block)
            pltpu.make_async_remote_copy(
                src_ref=xin.at[f, block], dst_ref=xin.at[f, block], send_sem=send_f,
                recv_sem=recv_a.at[f, block], device_id=(i, sibling), device_id_type=MESH,
            ).start()

    def send_first(f, targets):
        slot = i * 4 + y if f == 0 else 64 + i * 2 + pair
        for place_y, dz in targets:
            chip = (y + place_y) % 4 if f == 0 else member * 2 + place_y
            for k in range(2):
                for dc in range(2):
                    to_x, to_z = (x + 1 + core + 2 * k) % 4, (z + dz) % 4
                    dj = chip * 2 + (core + dc) % 2
                    src = first_out.at[f, dj, to_x // 2 * 4 + to_z]
                    copy = pltpu.make_async_remote_copy(
                        src_ref=src, dst_ref=recv_t.at[slot], send_sem=send_b.at[f],
                        recv_sem=recv_b.at[f], device_id=(to_x * 4 + to_z, dj), device_id_type=MESH,
                    )
                    if dz or dc or k == 0 or (f == 0 and place_y):
                        copy.start()
                    else:
                        here = jnp.logical_and(core == 1, chip == y)
                        pl.when(jnp.logical_not(here))(copy.start)
                        pl.when(here)(pltpu.make_async_copy(src, recv_t.at[slot], recv_b.at[f]).start)

    def spatial(f):
        heads, wide = (8, 640) if f == 0 else (4, 384)
        share = core if f == 0 else member * 2 + core
        features = heads * HD
        lane_gap = 512 if f == 0 else 256
        frame = i * 6 + (y if f == 0 else 4 + pair)
        own_clip = jnp.sum(jnp.where(lane96 == frame, clip_row, 0), axis=1, keepdims=True)

        def own_mod(n):
            picked = jnp.zeros((1, D), F32)
            for c in range(4):
                picked = jnp.where(own_clip == c, mod[n, c : c + 1, :], picked)
            return picked

        shift, scale, gate = own_mod(0), own_mod(1), own_mod(2)

        def place(h):
            low = share * (features - lane_gap) + h * HD
            return low, pl.multiple_of(jnp.minimum(low // 128, wide // 128 - 2) * 128, 128)

        arrived(f, j)
        if f == 1:
            for copy in head_columns(1):
                copy.wait()

        def project_chip(s, e):
            yy = (y + jnp.where(s == 0, 0, jnp.where(s == 1, 2, jnp.where(s == 2, 1, 3)))) % 4

            if f == 0:
                @pl.when(s == 1)
                def _():
                    for _ in range(4):
                        pltpu.make_async_copy(tokens.at[0], xin.at[0, 0], send_a.at[0]).wait()
                    send_tokens(1)
                    forward(0)

            arrived(f, yy * 2 + 1 - core)
            rows = xin[f, pl.ds(2 * yy, 2)].astype(F32).reshape(256, D)
            hidden = normed(rows, shift, scale)
            at = pl.ds(pl.multiple_of(yy * 256, 256), 256)

            qkv = dot(hidden, ws[:, : 3 * wide])
            q = (qkv[:, :wide] * Q_SCALE).reshape(2, 2, 2, 32, wide)
            for par in range(2):
                qtf[2 * e + par, :wide] = q[:, :, par].reshape(128, wide).T
                start = par * 512 + yy * 128 if f == 0 else yy // 2 * 512 + par * 256 + yy % 2 * 128
                cols = pl.ds(pl.multiple_of(start, 128), 128)
                for h in range(heads):
                    low, off = place(h)
                    row = lax.broadcasted_iota(jnp.int32, (WIN, 1), 0) + (off - low)
                    inside = jnp.logical_and(row >= 0, row < HD)
                    qt_s[h, :, cols] = jnp.where(inside, qtf[2 * e + par, pl.ds(off, WIN), :], 0.0).astype(BF16)
            k_s[at, :wide] = qkv[:, wide : 2 * wide].astype(BF16)
            vtf[e, :wide] = qkv[:, 2 * wide :].T
            for h in range(heads):
                low, _ = place(h)
                vt_s[h, :HD, at] = vtf[e, pl.ds(pl.multiple_of(low, 8), HD), :].astype(BF16)

        @pl.loop(0, 4 if f == 0 else 2)
        def _(u):
            if f == 0:
                project_chip(u, 0)
            else:
                project_chip(2 * u, 0)
                project_chip(2 * u + 1, 1)

        if f == 0:
            for copy in head_columns(1):
                copy.start()

        own_rows = pl.ds(pl.multiple_of(share * features, features), features)
        mix_f = mix_0 if f == 0 else mix_1

        def hand_over(src, dest, rows=own_rows):
            pltpu.make_async_remote_copy(
                src_ref=src, dst_ref=mix_f.at[rows], send_sem=send_m.at[f], recv_sem=recv_m.at[f],
                device_id=(i, dest), device_id_type=MESH,
            ).start()

        @pl.loop(0, 2)
        def _(n):
            block = (x + n - core + 2) % 2 if f == 0 else (member + 1 + n) % 2
            cols = pl.ds(pl.multiple_of(block * 512, 512), 512)

            def scores(h, buf):
                _, off = place(h)
                score[buf] = dot(k_s[:, pl.ds(off, WIN)], qt_s[h, :, cols])

            def attend(h, buf):
                values = score[buf]
                top = jnp.max(values, axis=0, keepdims=True)
                power[buf] = jnp.exp2(values - top).astype(BF16)
                out = dot(vt_s[h], power[buf])
                mixt[pl.ds(pl.multiple_of(h * HD, 8), HD), :] = out[:HD] * (1.0 / out[HD : HD + 1])

            scores(0, 0)

            several = 4 if f == 0 else 2

            @pl.loop(0, heads // several)
            def _(u):
                for e in range(several):
                    scores(jnp.minimum(several * u + e + 1, heads - 1), (e + 1) % 2)
                    attend(several * u + e, e % 2)

                if f == 1:
                    @pl.when(n == 0)
                    def _():
                        done = pl.ds(pl.multiple_of(u * 2 * HD, 2 * HD), 2 * HD)
                        rows = pl.ds(pl.multiple_of(share * features + u * 2 * HD, 2 * HD), 2 * HD)
                        for par in range(2):
                            mix_out_1[par, done, :] = mixt[done, par * 256 : par * 256 + 256].astype(BF16)
                            to_core = (par + x + 1) % 2
                            hand_over(mix_out_1.at[par, done], (y + 1 - 2 * member) * 2 + to_core, rows)

            if f == 0:
                @pl.when(n == 0)
                def _():
                    mix_out_0[...] = mixt[...].astype(BF16)
                    hand_over(mix_out_0, sibling)

                @pl.when(n == 1)
                def _():
                    mix_0[own_rows, :] = mixt[...].astype(BF16)
            else:
                for par in range(2):
                    part = mixt[:features, par * 256 : par * 256 + 256].astype(BF16)
                    to_core = (par + x + 1) % 2

                    @pl.when(jnp.logical_and(n == 1, to_core == core))
                    def _(part=part):
                        mix_1[own_rows, :] = part

                    @pl.when(jnp.logical_and(n == 1, to_core != core))
                    def _(part=part):
                        mix_out_1[2] = part
                        hand_over(mix_out_1.at[2], sibling)

        if f == 0:
            forward(1)
        arriving = mix_out_0 if f == 0 else mix_out_1
        pltpu.make_async_copy(arriving, arriving, recv_m.at[f]).wait()
        par = (x + core + 1) % 2

        def finish(b, mixed):
            proj = dot(mixed.astype(F32).T.astype(BF16), wo[...]).reshape(4, 2, 32, D)
            devs = pl.ds(4 * b, 4)
            for a in range(2):
                at = pl.ds(pl.multiple_of(a * 64 + par * 32, 32), 32)
                first = xin[f, devs, at, :].astype(F32) + gate * proj[:, a]
                first_out[f, devs, a * 4 : a * 4 + 4] = first.reshape(4, 4, 8, D).astype(BF16)

        if f == 0:
            @pl.loop(0, 2)
            def _(b):
                finish(b, mix_0[:, pl.ds(pl.multiple_of(b * 256, 256), 256)])

            pl.semaphore_wait(all_in, 7)
            send_first(0, YZ_FAR_FIRST)
        else:
            finish(member, mix_1[...])
            send_first(1, [(e, dz) for dz in (2, 1, 3, 0) for e in range(2)])

    lane96 = lax.broadcasted_iota(jnp.int32, (1, 96), 1)
    spatial(0)
    spatial(1)

    parts = ((0, 64, rows_a, qkv_a), (64, 32, rows_b, qkv_b))

    for f, (base, n, rows_f, qkv_f) in enumerate(parts):
        slots = recv_t.at[pl.ds(base, n)]
        pltpu.make_async_copy(slots, slots, recv_b.at[f]).wait()

        @pl.loop(0, n // 8)
        def _(c, base=base):
            rows = recv_t[pl.ds(base + c * 8, 8)].astype(F32).reshape(64, D)
            for b in range(9):
                f32_t[b, pl.ds(pl.multiple_of(base * 8 + c * 64, 64), 64), :] = rows[:, b * 128 : b * 128 + 128]

        @pl.loop(0, 8, unroll=4)
        def _(p, base=base, n=n, rows_f=rows_f):
            rows = jnp.concatenate([f32_t[b, pl.ds(base * 8 + p, n, stride=8), :] for b in range(9)], axis=1)
            at = pl.ds(pl.multiple_of(p * n, n), n)
            rows_f[at, :] = normed(rows, mods_t[0, base : base + n, :], mods_t[1, base : base + n, :])

        hidden = rows_f[...]
        qkv_f[:, :D] = (dot(hidden, wq[:, :D]) * Q_SCALE).astype(BF16)
        qkv_f[:, D:] = dot(hidden, wq[:, D:]).astype(BF16)

    same = clip_col == clip_slots

    def attend_position(p):
        at_a = pl.ds(pl.multiple_of(p * 64, 64), 64)
        at_b = pl.ds(pl.multiple_of(p * 32, 32), 32)
        blocks = [jnp.zeros((96, 128), F32) for _ in range(9)]
        for h in range(HEADS):
            off = window(h)
            lane = lax.broadcasted_iota(jnp.int32, (1, WIN), 1) + (off - h * HD)
            inside = jnp.logical_and(lane >= 0, lane < HD)

            def part(m):
                cols = slice(m * D + off, m * D + off + WIN)
                return jnp.concatenate([qkv_a[at_a, cols], qkv_b[at_b, cols]], axis=0)

            q = part(0)
            q = jnp.where(inside, q, jnp.zeros_like(q))
            scores = jnp.where(same, dot_t(q, part(1)), NEG)
            powers = jnp.exp2(scores - jnp.max(scores, axis=-1, keepdims=True))
            total = jnp.sum(powers, axis=-1, keepdims=True)
            out = dot(powers.astype(BF16), part(2)) * (1.0 / total)
            for b in range(off // 128, off // 128 + 2):
                lanes = slice(b * 128 - off, b * 128 - off + 128)
                blocks[b] = jnp.where(inside[:, lanes], out[:, lanes], blocks[b])
        for b in range(9):
            cols = slice(b * 128, b * 128 + 128)
            rows_a[at_a, cols] = blocks[b][:64].astype(BF16)
            rows_b[at_b, cols] = blocks[b][64:].astype(BF16)

    @pl.loop(0, 4)
    def _(u):
        attend_position(2 * u)
        attend_position(2 * u + 1)

    for f, (base, n, rows_f, _) in enumerate(parts):
        proj = dot(rows_f[...], wo2[...])
        for p in range(8):
            at = pl.ds(base * 8 + p, n, stride=8)
            for b in range(9):
                cols = slice(b * 128, b * 128 + 128)
                f32_t[b, at, :] = f32_t[b, at, :] + mods_t[2, base : base + n, cols] * proj[p * n : p * n + n, cols]

        @pl.loop(0, n // 8)
        def _(c, base=base):
            at = pl.ds(pl.multiple_of(base * 8 + c * 64, 64), 64)
            rows = jnp.concatenate([f32_t[b, at, :] for b in range(9)], axis=1)
            recv_t[pl.ds(base + c * 8, 8)] = rows.reshape(8, 8, D).astype(BF16)

        size, start = (4, 0) if f == 0 else (2, 4)
        for dx, dz in XZ_FAR_FIRST:
            di = (x + dx) % 4 * 4 + (z + dz) % 4
            pltpu.make_async_remote_copy(
                src_ref=recv_t.at[pl.ds(base + di * size, size)], dst_ref=final.at[pl.ds(start, size), i],
                send_sem=send_c, recv_sem=recv_c, device_id=(di, j), device_id_type=MESH,
            ).start()
        src = recv_t.at[pl.ds(base + i * size, size)]
        pltpu.make_async_copy(src, final.at[pl.ds(start, size), i], recv_c).start()

    for _ in range(4):
        pltpu.make_async_copy(tokens.at[0], xin.at[0, 0], send_a.at[1]).wait()
    for _ in range(6):
        pltpu.make_async_copy(tokens.at[0], xin.at[0, 0], send_f).wait()
    pltpu.make_async_copy(mix_out_0, mix_out_0, send_m.at[0]).wait()
    for _ in range(3):
        pltpu.make_async_copy(mix_out_1.at[0], mix_out_1.at[0], send_m.at[1]).wait()

    @pl.loop(0, 64 - core)
    def _(n):
        pltpu.make_async_copy(recv_t.at[0], recv_t.at[0], send_b.at[0]).wait()

    self_sent = jnp.where(jnp.logical_and(core == 1, pair == member), 1, 0)

    @pl.loop(0, 32 - self_sent)
    def _(n):
        pltpu.make_async_copy(recv_t.at[0], recv_t.at[0], send_b.at[1]).wait()

    @pl.loop(0, 15)
    def _(n):
        pltpu.make_async_copy(recv_t.at[pl.ds(0, 6)], recv_t.at[pl.ds(0, 6)], send_c).wait()

    pltpu.make_async_copy(final, final, recv_c).wait()


def copy_kernel(src, out, buf, in_sem, out_sem):
    ins = [pltpu.make_async_copy(src.at[n], buf.at[n], in_sem.at[n]) for n in range(6)]
    outs = [pltpu.make_async_copy(buf.at[n], out.at[n], out_sem.at[n]) for n in range(6)]
    for copy in ins:
        copy.start()
    for arriving, leaving in zip(ins, outs):
        arriving.wait()
        leaving.start()
    for copy in outs:
        copy.wait()


def body(tokens, clip_ids, modulation, w_spatial_qkv, w_spatial_out, w_temporal_qkv, w_temporal_out):
    any_, vmem = pl.BlockSpec(memory_space=pl.ANY), pl.BlockSpec(memory_space=pltpu.VMEM)
    dma = pltpu.SemaphoreType.DMA
    final = pl.pallas_call(
        kernel,
        out_shape=jax.ShapeDtypeStruct((6, 16, 8, D), BF16),
        in_specs=[any_, vmem, vmem, any_, any_, any_, any_],
        out_specs=any_,
        scratch_shapes=[
            pltpu.VMEM((2, 8, 128, D), BF16),
            pltpu.VMEM((D, 3 * D), BF16),
            pltpu.VMEM((D, 1920), BF16),
            pltpu.VMEM((D, D), BF16),
            pltpu.VMEM((D, D), BF16),
            pltpu.VMEM((4, 640, 128), F32),
            pltpu.VMEM((2, 640, 256), F32),
            pltpu.VMEM((HEADS // 2, WIN, 1024), BF16),
            pltpu.VMEM((1024, 640), BF16),
            pltpu.VMEM((HEADS // 2, HD + 8, 1024), BF16),
            pltpu.VMEM((2, 1024, 512), F32),
            pltpu.VMEM((2, 1024, 512), BF16),
            pltpu.VMEM((D // 2, 512), F32),
            pltpu.VMEM((D // 2, 512), BF16),
            pltpu.VMEM((3, D // 4, 256), BF16),
            pltpu.VMEM((D, 512), BF16),
            pltpu.VMEM((D, 256), BF16),
            pltpu.VMEM((2, 8, 8, 8, D), BF16),
            pltpu.VMEM((96, 8, D), BF16),
            pltpu.VMEM((9, 768, 128), F32),
            pltpu.VMEM((512, D), BF16),
            pltpu.VMEM((256, D), BF16),
            pltpu.VMEM((512, 3 * D), BF16),
            pltpu.VMEM((256, 3 * D), BF16),
            pltpu.VMEM((3, 96, D), F32),
            dma((2,)), dma((2, 8)), dma, dma((2,)), dma((2,)), dma((2,)), dma((2,)), dma, dma, dma((9,)),
            pltpu.SemaphoreType.REGULAR,
        ],
        compiler_params=pltpu.CompilerParams(
            collective_id=0, has_side_effects=True, vmem_limit_bytes=63 * 1024 * 1024
        ),
        name="block",
    )(
        tokens, clip_ids.reshape(1, 96), modulation.transpose(1, 0, 2),
        w_spatial_qkv, w_spatial_out, w_temporal_qkv, w_temporal_out,
    )
    return pl.pallas_call(
        copy_kernel,
        out_shape=jax.ShapeDtypeStruct((6, 128, D), BF16),
        in_specs=[any_],
        out_specs=any_,
        scratch_shapes=[pltpu.VMEM((6, 128, D), BF16), dma((6,)), dma((6,))],
        compiler_params=pltpu.CompilerParams(vmem_limit_bytes=63 * 1024 * 1024),
        name="result",
    )(final.reshape(6, 128, D))


def solution(mesh):
    in_specs = (P("frame", "inframe", None), P(), P(), P(), P(), P(), P())
    out_specs = P("frame", "inframe", None)
    return jax.shard_map(body, mesh=mesh, in_specs=in_specs, out_specs=out_specs, check_vma=False)
```
